512 devices in a mesh: rep: 16 (over x, z_hi, core), tab: 32 (over y, z_lo).
Axes of the slice: x: 4, y: 4, z: 16 (z_hi: 2, z_lo: 8; z = z_hi * 8 + z_lo), core: 2. Of those that a mesh axis runs over, the one named last changes fastest.
Arguments:
- bottom_out: bfloat16 [65536, 128], P(('rep', 'tab')), may hold values from -1.5 to 1.5
- pooled: bfloat16 [65536, 32, 128], P(('rep', 'tab')), may hold values from -1.5 to 1.5
- top_grad: bfloat16 [65536, 512], P(('rep', 'tab')), may hold values from -6 to 6
- top_weight: bfloat16 [656, 512], replicated, may hold values from -0.25 to 0.25
- core_first: bfloat16 [32, 128, 256], P('tab'), may hold values from -4 to 4
- core_mid: bfloat16 [32, 16, 64, 256], P('tab'), may hold values from -0.75 to 0.75
- core_last: bfloat16 [32, 128, 512], P('tab'), may hold values from -0.75 to 0.75
- digit_first: int32 [32, 65536], P('tab', 'rep'), may hold values from 0 to 127
- digit_last: int32 [32, 65536], P('tab', 'rep'), may hold values from 0 to 127
- grouped: int32 [32, 16, 4096], P('tab', 'rep'), may hold values from 0 to 4095, each once within a row
Outputs:
- grad_first: float32 [32, 128, 256], P('tab', 'rep')
- grad_mid: float32 [32, 16, 64, 256], P('tab', 'rep')
- grad_last: float32 [32, 128, 512], P('tab', 'rep')
- grad_top: bfloat16 [656, 512], replicated
- grad_bottom: bfloat16 [65536, 128], P(('rep', 'tab'))
The draws below stay inside these ranges and needn't reach their ends.
Inputs may be any that keep to these rules, and one draw needn't show every extreme that they name: `grouped`: for each table and rep group, a permutation of the 4096 positions of that group's samples; the sample at position p has second digit p // 256, so every second digit has exactly 256 samples in each rep group.
All inputs are finite; a program needn't handle non-finite values.
Results may differ from the reference program's by a relative error of at most 0.017.
Values may be sent and summed in bfloat16 or wider, within the bound.
No kernel may reach another device: no remote copies, remote signals or barrier semaphores. Data moves between devices by JAX's collectives and lax.ppermute only.
A program may use at most 64 MiB of HBM per device.

```python
import jax
import jax.numpy as jnp
import numpy as np
from jax import lax

D1 = 4
D2 = 4
D3 = 8
D = 128
R = 64
I1 = 128
I2 = 16
I3 = 128
H = 512
SAMP = 128
TABLES = 32
P_SIZE = 528
BATCH = 65536
NS = 4096
N_REP = 16


def plant(drawn, own_key, least, top_value):
    shape = drawn.shape
    place = [jax.random.randint(jax.random.fold_in(own_key, axis), (), 0, shape[axis]) for axis in range(len(shape))]
    drawn = drawn.at[tuple(place)].set(least)
    longest = shape.index(max(shape))
    place[longest] = (place[longest] + 1) % shape[longest]
    return drawn.at[tuple(place)].set(top_value)


def block_scale(own_key, shape, shards, smallest, top_value):
    def one(axis_at, blocks):
        steps = jax.random.uniform(jax.random.fold_in(jax.random.fold_in(own_key, 6), axis_at), (blocks,), jnp.float32, smallest / len(shards), top_value / len(shards))
        return jnp.repeat(jnp.exp(steps), shape[axis_at] // blocks).reshape((-1,) + (1,) * (len(shape) - axis_at - 1))

    factor_of = one(*shards[0])
    for cut in shards[1:]:
        factor_of = factor_of * one(*cut)
    return factor_of


def noise(stream_key, shape, deviation, most, cuts=(), dtype=jnp.bfloat16):
    factor_of = block_scale(stream_key, shape, cuts, -0.22, 0.18) if cuts else 1.0
    array = jax.random.normal(stream_key, shape, jnp.float32) * deviation * factor_of
    return jnp.minimum(jnp.maximum(array, -most), most).astype(dtype)


def setup_inputs(seed: int = 0) -> dict:
    splits = jax.random.split(jax.random.key(seed), 11)
    return {
        "bottom_out": noise(splits[0], (BATCH, D), 0.25, 1.5, ((0, 512),)),
        "pooled": noise(splits[1], (BATCH, TABLES, D), 0.25, 1.5, ((0, 512),)),
        "top_grad": noise(splits[2], (BATCH, H), 1.0, 6.0, ((0, 512),)),
        "top_weight": noise(splits[3], (D + P_SIZE, H), (D + P_SIZE) ** -0.5, 0.25),
        "core_first": noise(splits[4], (TABLES, I1, D1 * R), 1.0, 4.0, ((0, 32),)),
        "core_mid": noise(splits[5], (TABLES, I2, R, D2 * R), R ** -0.5, 0.75, ((0, 32),)),
        "core_last": noise(splits[6], (TABLES, I3, D3 * R), R ** -0.5, 0.75, ((0, 32),)),
        "digit_first": plant(jax.random.randint(splits[7], (TABLES, BATCH), 0, I1), jax.random.fold_in(splits[7], 1), 0, I1 - 1).astype(jnp.int32),
        "digit_last": plant(jax.random.randint(splits[8], (TABLES, BATCH), 0, I3), jax.random.fold_in(splits[8], 1), 0, I3 - 1).astype(jnp.int32),
        "grouped": jax.vmap(lambda own: jax.random.permutation(own, NS))(jax.random.split(splits[9], TABLES * N_REP)).reshape((TABLES, N_REP, NS)).astype(jnp.int32),
    }


def dense_block(carry, blocks, top_weight, lower_rows, lower_cols, scale):
    bottom_rows, pooled_rows, grad_block = blocks
    features = jnp.concatenate([bottom_rows[:, None, :], pooled_rows], axis=1)
    feat_wide = features.astype(jnp.float32)
    gram = jnp.einsum('bid,bjd->bij', feat_wide, feat_wide)
    pairs = gram[:, lower_rows, lower_cols]
    inputs = jnp.concatenate([bottom_rows.astype(jnp.float32), pairs], axis=1).astype(jnp.bfloat16)
    carry = carry + scale * lax.dot_general(inputs, grad_block, (((0,), (0,)), ((), ())), preferred_element_type=jnp.float32)
    grad_inputs = lax.dot_general(grad_block, top_weight, (((1,), (1,)), ((), ())), preferred_element_type=jnp.float32)
    width = bottom_rows.shape[1]
    count = features.shape[1]
    sym = jnp.zeros((features.shape[0], count, count), jnp.float32)
    sym = sym.at[:, lower_rows, lower_cols].set(grad_inputs[:, width:])
    sym = sym + jnp.swapaxes(sym, 1, 2)
    grad_features = jnp.einsum('bij,bjd->bid', sym, feat_wide)
    grad_bottom = (grad_inputs[:, :width] + grad_features[:, 0]).astype(jnp.bfloat16)
    grad_rows = grad_features[:, 1:].astype(jnp.bfloat16)
    return (carry, (grad_bottom, grad_rows))

def table_partial(grads, order, first_digit, third_digit, core_one, core_two, core_three):
    samples = grads.shape[0]
    group = samples // I2
    picked = grads[order].astype(jnp.float32).reshape(I2, group, D1, D2, D3)
    first = first_digit[order]
    third = third_digit[order]
    left_core = core_one[first].astype(jnp.float32).reshape(I2, group, D1, R)
    right_core = core_three[third].astype(jnp.float32).reshape(I2, group, D3, R)
    mid_core = core_two.astype(jnp.float32).reshape(I2, R, D2, R)
    inner = jnp.einsum('kgabc,kgcs->kgabs', picked, right_core).astype(jnp.bfloat16)
    inner = lax.optimization_barrier(inner).astype(jnp.float32)
    grad_two = jnp.einsum('kgar,kgabs->krbs', left_core, inner).reshape(I2, R, D2 * R)
    back_first = jnp.einsum('kgabs,krbs->kgar', inner, mid_core).astype(jnp.bfloat16)
    chained = jnp.einsum('kgar,krbs->kgabs', left_core, mid_core).astype(jnp.bfloat16)
    chained = lax.optimization_barrier(chained).astype(jnp.float32)
    back_last = jnp.einsum('kgabc,kgabs->kgcs', picked, chained).astype(jnp.bfloat16)
    grad_one = jax.ops.segment_sum(back_first.reshape(samples, D1 * R).astype(jnp.float32), first, num_segments=I1)
    grad_three = jax.ops.segment_sum(back_last.reshape(samples, D3 * R).astype(jnp.float32), third, num_segments=I3)
    return (grad_one, grad_two, grad_three)

def reference(bottom_out, pooled, top_grad, top_weight, core_first, core_mid, core_last, digit_first, digit_last, grouped):
    batch_all = bottom_out.shape[0]
    tables = pooled.shape[1]
    count = tables + 1
    lower_rows, lower_cols = np.tril_indices(count, -1)
    scale = jnp.float32(1.0 / np.sqrt(batch_all))
    blocks = batch_all // SAMP
    xs = (bottom_out.reshape(blocks, SAMP, D), pooled.reshape(blocks, SAMP, tables, D), top_grad.reshape(blocks, SAMP, -1))
    init = jnp.zeros((top_weight.shape[0], top_weight.shape[1]), jnp.float32)
    total, (grad_bottom, grad_rows) = lax.scan(lambda carry, blk: dense_block(carry, blk, top_weight, lower_rows, lower_cols, scale), init, xs)
    grad_bottom = grad_bottom.reshape(batch_all, D)
    reps = grouped.shape[1]
    group_size = grouped.shape[2]
    grad_rows = grad_rows.reshape(reps, group_size, tables, D).transpose(2, 0, 1, 3)
    first_all = digit_first.reshape(tables, reps, group_size)
    last_all = digit_last.reshape(tables, reps, group_size)

    def per_table(items):
        grads_t, order_t, first_t, last_t, one_t, two_t, three_t = items

        def per_group(acc, inner_items):
            grads_q, order_q, first_q, last_q = inner_items
            parts = table_partial(grads_q, order_q, first_q, last_q, one_t, two_t, three_t)
            return ((acc[0] + parts[0], acc[1] + parts[1], acc[2] + parts[2]), None)
        zeros = (jnp.zeros((I1, D1 * R), jnp.float32), jnp.zeros((I2, R, D2 * R), jnp.float32), jnp.zeros((I3, D3 * R), jnp.float32))
        sums, unused = lax.scan(per_group, zeros, (grads_t, order_t, first_t, last_t))
        return sums
    grad_one, grad_two, grad_three = lax.map(per_table, (grad_rows, grouped, first_all, last_all, core_first, core_mid, core_last))
    return (scale * grad_one, scale * grad_two, scale * grad_three, total.astype(jnp.bfloat16), grad_bottom)
```

```python
import jax
import jax.numpy as jnp
import numpy as np
from jax import lax
from jax.experimental import pallas as pl
from jax.experimental.pallas import tpu as pltpu
from jax.sharding import PartitionSpec as P

D1 = 4
D2 = 4
D3 = 8
R = 64
I1 = 128
I2 = 16
I3 = 128
LANES = 128
SUB = 8
BF = jnp.bfloat16
F32 = jnp.float32
NT = (((1,), (1,)), ((), ()))
TN = (((0,), (0,)), ((), ()))
NN = (((1,), (0,)), ((), ()))


def pair(i, j):
    low, high = min(i, j), max(i, j)
    return high * (high - 1) // 2 + low


def dense_kernel(count, bottom_ref, pooled_ref, grad_ref, weight_ref, rows_ref, gbottom_ref, feat_ref, wide, feat, gi, out):
    samples, width = bottom_ref.shape
    tables = count - 1
    gi[...] = lax.dot_general(weight_ref[...], grad_ref[...], NT, preferred_element_type=F32)
    wide[...] = pooled_ref[...].astype(F32)
    feat[0] = bottom_ref[...].astype(F32).T
    for t in range(tables):
        feat[1 + t] = wide[pl.ds(t, samples, stride=tables), :].T
    feat_ref[...] = feat[...].astype(BF)

    def chunk(step, carry):
        at = pl.ds(pl.multiple_of(step * SUB, SUB), SUB)
        parts = [feat[j, at, :] for j in range(count)]
        for i in range(count):
            total = None
            for j in range(count):
                if j != i:
                    row = gi[pl.ds(width + pair(i, j), 1), :]
                    term = jnp.broadcast_to(row, (SUB, samples)) * parts[j]
                    total = term if total is None else total + term
            out[i, at, :] = total
        return carry

    lax.fori_loop(0, width // SUB, chunk, 0)
    gbottom_ref[...] = (out[0] + gi[pl.ds(0, width), :]).T.astype(BF)
    for t in range(tables):
        rows_ref[t] = out[1 + t].T.astype(BF)


def gram_kernel(count, scale, feat_ref, grad_ref, top_ref, feat, pairs):
    width, samples = feat_ref.shape[1:]
    feat[...] = feat_ref[...].astype(F32)
    for i0 in range(0, count, 4):
        for j0 in range(0, count, 8):
            todo = [(i, j) for i in range(i0, min(i0 + 4, count)) for j in range(j0, min(j0 + 8, count)) if j < i]
            if not todo:
                continue
            used = sorted({i for one in todo for i in one})

            def chunk(step, totals, todo=todo, used=used):
                at = pl.ds(pl.multiple_of(step * SUB, SUB), SUB)
                parts = {i: feat[i, at, :] for i in used}
                return tuple(total + parts[i] * parts[j] for total, (i, j) in zip(totals, todo))

            zero = jnp.zeros((SUB, samples), F32)
            totals = lax.fori_loop(0, width // SUB, chunk, (zero,) * len(todo), unroll=2)
            for total, (i, j) in zip(totals, todo):
                pairs[pl.ds(pair(i, j), 1), :] = jnp.sum(total, axis=0, keepdims=True)
    top_ref[:width] = scale * lax.dot_general(feat_ref[0], grad_ref[...], NN, preferred_element_type=F32)
    top_ref[width:] = scale * lax.dot_general(pairs[...].astype(BF), grad_ref[...], NN, preferred_element_type=F32)


def digits_kernel(order_ref, first_ref, last_ref, sorted_ref):
    order = order_ref[...]
    both = first_ref[...] * I3 + last_ref[...]
    row, lane = order // LANES, order % LANES
    total = jnp.zeros(order.shape, jnp.int32)
    for r in range(order.shape[0]):
        spread = jnp.broadcast_to(both[r : r + 1], order.shape)
        total = jnp.where(row == r, jnp.take_along_axis(spread, lane, axis=1), total)
    sorted_ref[...] = total


def onehot(digit, slots):
    lanes = digit.shape[1]
    return jnp.where(lax.broadcasted_iota(jnp.int32, (slots, lanes), 0) == digit, 1.0, 0.0).astype(BF)


def digits_of(sorted_ref, group):
    rows = group // LANES
    at = sorted_ref[pl.ds(pl.program_id(0) * rows, rows), :]
    at = jnp.concatenate([at[r : r + 1] for r in range(rows)], axis=1)
    return at // I3, at % I3


def before_kernel(sorted_ref, one_ref, mid_ref, three_ref, left_ref, right_ref, chained_ref):
    group = left_ref.shape[1]
    first, third = digits_of(sorted_ref, group)
    left = lax.dot_general(one_ref[...], onehot(first, I1), NN, preferred_element_type=F32).astype(BF)
    left_ref[...] = left
    right_ref[...] = lax.dot_general(three_ref[...], onehot(third, I3), NN, preferred_element_type=F32).astype(BF)
    for a in range(D1):
        chained = lax.dot_general(mid_ref[0], left[a * R : (a + 1) * R], TN, preferred_element_type=F32)
        chained_ref[a * D2 * R : (a + 1) * D2 * R] = chained.astype(BF)


def after_kernel(scale, order_ref, sorted_ref, received_ref, left_ref, right_ref, chained_ref, mid_ref, one_ref, two_ref, three_ref, wide, picked, gt, inner, back, acc_one, acc_three, right_wide, chained_wide):
    k = pl.program_id(0)
    groups = pl.num_programs(0)
    group = left_ref.shape[1]
    steps = (R // SUB) * (group // LANES)
    share = group // steps

    def fetch(slot, base, begin, number):
        for n in range(number):
            picked[slot, pl.ds(begin + n, 1), :] = wide[pl.ds(order_ref[base + begin + n], 1), :]

    @pl.when(k == 0)
    def _():
        wide[...] = received_ref[...].astype(F32)
        acc_one[...] = jnp.zeros_like(acc_one)
        acc_three[...] = jnp.zeros_like(acc_three)

        def one(step, carry):
            fetch(0, 0, step * share, share)
            return carry

        lax.fori_loop(0, steps, one, 0)

    slot = k % 2
    later = jnp.minimum(k + 1, groups - 1) * group
    gt[...] = picked[slot].T
    right_wide[...] = right_ref[...].astype(F32)
    chained_wide[...] = chained_ref[...].astype(F32)

    def chunk(step, carry):
        fetch(1 - slot, later, step * share, share)
        half = step // (R // SUB)
        lanes = pl.ds(pl.multiple_of(half * LANES, LANES), LANES)
        low = (step % (R // SUB)) * SUB
        rights = [right_wide[pl.ds(pl.multiple_of(c * R + low, SUB), SUB), lanes] for c in range(D3)]
        totals = [None] * D3
        for j in range(D1 * D2):
            at = pl.ds(pl.multiple_of(j * R + low, SUB), SUB)
            link = chained_wide[at, lanes]
            total = None
            for c in range(D3):
                g = jnp.broadcast_to(gt[pl.ds(j * D3 + c, 1), lanes], (SUB, LANES))
                term = g * rights[c]
                total = term if total is None else total + term
                term = g * link
                totals[c] = term if totals[c] is None else totals[c] + term
            inner[at, lanes] = total
        for c in range(D3):
            back[pl.ds(pl.multiple_of(c * R + low, SUB), SUB), lanes] = totals[c]
        return carry

    lax.fori_loop(0, steps, chunk, 0)
    first, third = digits_of(sorted_ref, group)
    inner_all = inner[...].astype(BF)
    two = None
    firsts = []
    for a in range(D1):
        part = inner_all[a * D2 * R : (a + 1) * D2 * R]
        term = lax.dot_general(left_ref[a * R : (a + 1) * R], part, NT, preferred_element_type=F32)
        two = term if two is None else two + term
        firsts.append(lax.dot_general(mid_ref[0], part, NN, preferred_element_type=F32).astype(BF))
    two_ref[0] = (scale * two).astype(BF)
    back_first = jnp.concatenate(firsts, axis=0)
    acc_one[...] += lax.dot_general(onehot(first, I1), back_first, NT, preferred_element_type=F32)
    acc_three[...] += lax.dot_general(onehot(third, I3), back[...].astype(BF), NT, preferred_element_type=F32)

    @pl.when(k == groups - 1)
    def _():
        one_ref[...] = (scale * acc_one[...]).astype(BF)
        three_ref[...] = (scale * acc_three[...]).astype(BF)


def whole(shape):
    return pl.BlockSpec(shape, lambda *a: (0,) * len(shape))


def dense(bottom_out, pooled, top_grad, top_weight):
    samples, width = bottom_out.shape
    tables = pooled.shape[1]
    count = tables + 1
    return pl.pallas_call(
        lambda *refs: dense_kernel(count, *refs),
        out_shape=(
            jax.ShapeDtypeStruct((tables, samples, width), BF),
            jax.ShapeDtypeStruct((samples, width), BF),
            jax.ShapeDtypeStruct((count, width, samples), BF),
        ),
        scratch_shapes=[
            pltpu.VMEM((samples * tables, width), F32),
            pltpu.VMEM((count, width, samples), F32),
            pltpu.VMEM((top_weight.shape[0], samples), F32),
            pltpu.VMEM((count, width, samples), F32),
        ],
        compiler_params=pltpu.CompilerParams(vmem_limit_bytes=48 << 20),
        name="dense",
    )(bottom_out, pooled.reshape(samples * tables, width), top_grad, top_weight)


def gram(feat, top_grad, scale):
    count, width, samples = feat.shape
    pairs = count * (count - 1) // 2
    return pl.pallas_call(
        lambda *refs: gram_kernel(count, scale, *refs),
        out_shape=jax.ShapeDtypeStruct((width + pairs, top_grad.shape[1]), F32),
        scratch_shapes=[pltpu.VMEM((count, width, samples), F32), pltpu.VMEM((pairs, samples), F32)],
        compiler_params=pltpu.CompilerParams(vmem_limit_bytes=48 << 20),
        name="gram",
    )(feat, top_grad)


def before(order, first, last, core_one, core_two, core_three):
    total = order.shape[0]
    group = total // I2
    table = (total // LANES, LANES)
    sorted_digits = pl.pallas_call(
        digits_kernel, out_shape=jax.ShapeDtypeStruct(table, jnp.int32), name="digits"
    )(order.reshape(table), first.reshape(table), last.reshape(table))
    links = pl.pallas_call(
        before_kernel,
        grid=(I2,),
        in_specs=[
            whole(table),
            whole((D1 * R, I1)),
            pl.BlockSpec((1, R, D2 * R), lambda k: (k, 0, 0)),
            whole((D3 * R, I3)),
        ],
        out_specs=(
            pl.BlockSpec((D1 * R, group), lambda k: (0, k)),
            pl.BlockSpec((D3 * R, group), lambda k: (0, k)),
            pl.BlockSpec((D1 * D2 * R, group), lambda k: (0, k)),
        ),
        out_shape=(
            jax.ShapeDtypeStruct((D1 * R, total), BF),
            jax.ShapeDtypeStruct((D3 * R, total), BF),
            jax.ShapeDtypeStruct((D1 * D2 * R, total), BF),
        ),
        compiler_params=pltpu.CompilerParams(vmem_limit_bytes=48 << 20),
        name="before",
    )(sorted_digits, core_one.T, core_two, core_three.T)
    return sorted_digits, links


def after(received, order, sorted_digits, links, core_two, scale):
    total, width = received.shape
    group = total // I2
    left, right, chained = links
    return pl.pallas_call(
        lambda *refs: after_kernel(scale, *refs),
        grid_spec=pltpu.PrefetchScalarGridSpec(
            num_scalar_prefetch=1,
            grid=(I2,),
            in_specs=[
                whole(sorted_digits.shape),
                whole((total, width)),
                pl.BlockSpec((D1 * R, group), lambda k, o: (0, k)),
                pl.BlockSpec((D3 * R, group), lambda k, o: (0, k)),
                pl.BlockSpec((D1 * D2 * R, group), lambda k, o: (0, k)),
                pl.BlockSpec((1, R, D2 * R), lambda k, o: (k, 0, 0)),
            ],
            out_specs=(
                whole((I1, D1 * R)),
                pl.BlockSpec((1, R, D2 * R), lambda k, o: (k, 0, 0)),
                whole((I3, D3 * R)),
            ),
            scratch_shapes=[
                pltpu.VMEM((total, width), F32),
                pltpu.VMEM((2, group, width), F32),
                pltpu.VMEM((width, group), F32),
                pltpu.VMEM((D1 * D2 * R, group), F32),
                pltpu.VMEM((D3 * R, group), F32),
                pltpu.VMEM((I1, D1 * R), F32),
                pltpu.VMEM((I3, D3 * R), F32),
                pltpu.VMEM((D3 * R, group), F32),
                pltpu.VMEM((D1 * D2 * R, group), F32),
            ],
        ),
        out_shape=(
            jax.ShapeDtypeStruct((I1, D1 * R), BF),
            jax.ShapeDtypeStruct((I2, R, D2 * R), BF),
            jax.ShapeDtypeStruct((I3, D3 * R), BF),
        ),
        compiler_params=pltpu.CompilerParams(vmem_limit_bytes=48 << 20),
        name="after",
    )(order, sorted_digits, received, left, right, chained, core_two)


def scatter_sum(array):
    return lax.psum_scatter(array, "rep", scatter_dimension=0, tiled=True)


def on_device(
    bottom_out,
    pooled,
    top_grad,
    top_weight,
    core_first,
    core_mid,
    core_last,
    digit_first,
    digit_last,
    grouped,
):
    samples, width = bottom_out.shape
    reps = lax.axis_size("rep")
    batch_all = samples * reps * lax.axis_size("tab")
    scale = float(np.float32(1.0 / np.sqrt(batch_all)))
    grad_rows, grad_bottom, feat = dense(bottom_out, pooled, top_grad, top_weight)
    received = lax.all_to_all(grad_rows, "tab", split_axis=0, concat_axis=0, tiled=True)
    dense_term = gram(feat, top_grad, scale)
    grad_top = lax.psum(dense_term, ("rep", "tab")).astype(BF)
    order = grouped[0, 0]
    sorted_digits, links = before(
        order, digit_first[0], digit_last[0], core_first[0], core_mid[0], core_last[0]
    )
    one, two, three = after(
        received.reshape(-1, width), order, sorted_digits, links, core_mid[0], scale
    )
    parts = jnp.concatenate(
        [one.reshape(reps, -1, LANES), two.reshape(reps, -1, LANES), three.reshape(reps, -1, LANES)],
        axis=1,
    )
    share = scatter_sum(parts.reshape(-1, LANES)).astype(F32)
    size_one = I1 * D1 * R // reps // LANES
    size_two = I2 * R * D2 * R // reps // LANES
    grad_one = share[:size_one].reshape(1, I1 // reps, D1 * R)
    grad_two = share[size_one : size_one + size_two].reshape(1, I2 // reps, R, D2 * R)
    grad_three = share[size_one + size_two :].reshape(1, I3 // reps, D3 * R)
    return (grad_one, grad_two, grad_three, grad_top, grad_bottom)


def solution(mesh):
    return jax.shard_map(
        on_device,
        mesh=mesh,
        in_specs=(
            P(("rep", "tab"), None),
            P(("rep", "tab"), None, None),
            P(("rep", "tab"), None),
            P(),
            P("tab", None, None),
            P("tab", None, None, None),
            P("tab", None, None),
            P("tab", "rep"),
            P("tab", "rep"),
            P("tab", "rep", None),
        ),
        out_specs=(
            P("tab", "rep", None),
            P("tab", "rep", None, None),
            P("tab", "rep", None),
            P(),
            P(("rep", "tab"), None),
        ),
        check_vma=False,
    )
```

```python
import jax
import jax.numpy as jnp
import numpy as np
from jax import lax
from jax.experimental import pallas as pl
from jax.experimental.pallas import tpu as pltpu
from jax.sharding import PartitionSpec as P

D1 = 4
D2 = 4
D3 = 8
R = 64
I1 = 128
I2 = 16
I3 = 128
LANES = 128
SUB = 8
BF = jnp.bfloat16
F32 = jnp.float32
NT = (((1,), (1,)), ((), ()))
TN = (((0,), (0,)), ((), ()))
NN = (((1,), (0,)), ((), ()))


def pair(i, j):
    low, high = min(i, j), max(i, j)
    return high * (high - 1) // 2 + low


def dense_kernel(count, bottom_ref, pooled_ref, grad_ref, weight_ref, rows_ref, gbottom_ref, feat_ref, wide, feat, gi, out):
    samples, width = bottom_ref.shape
    tables = count - 1
    gi[...] = lax.dot_general(weight_ref[...], grad_ref[...], NT, preferred_element_type=F32)
    wide[...] = pooled_ref[...].astype(F32)
    feat[0] = bottom_ref[...].astype(F32).T
    for t in range(tables):
        feat[1 + t] = wide[pl.ds(t, samples, stride=tables), :].T
    feat_ref[...] = feat[...].astype(BF)

    def chunk(step, carry):
        at = pl.ds(pl.multiple_of(step * SUB, SUB), SUB)
        parts = [feat[j, at, :] for j in range(count)]
        for i in range(count):
            total = None
            for j in range(count):
                if j != i:
                    row = gi[pl.ds(width + pair(i, j), 1), :]
                    term = jnp.broadcast_to(row, (SUB, samples)) * parts[j]
                    total = term if total is None else total + term
            out[i, at, :] = total
        return carry

    lax.fori_loop(0, width // SUB, chunk, 0)
    gbottom_ref[...] = (out[0] + gi[pl.ds(0, width), :]).T.astype(BF)
    for t in range(tables):
        rows_ref[t] = out[1 + t].T.astype(BF)


def gram_kernel(count, scale, at_ref, feat_ref, grad_ref, keep_ref, send_ref, feat, pairs, top):
    width, samples = feat_ref.shape[1:]
    feat[...] = feat_ref[...].astype(F32)
    for i0 in range(0, count, 4):
        for j0 in range(0, count, 8):
            todo = [(i, j) for i in range(i0, min(i0 + 4, count)) for j in range(j0, min(j0 + 8, count)) if j < i]
            if not todo:
                continue
            used = sorted({i for one in todo for i in one})

            def chunk(step, totals, todo=todo, used=used):
                at = pl.ds(pl.multiple_of(step * SUB, SUB), SUB)
                parts = {i: feat[i, at, :] for i in used}
                return tuple(total + parts[i] * parts[j] for total, (i, j) in zip(totals, todo))

            zero = jnp.zeros((SUB, samples), F32)
            totals = lax.fori_loop(0, width // SUB, chunk, (zero,) * len(todo), unroll=2)
            for total, (i, j) in zip(totals, todo):
                pairs[pl.ds(pair(i, j), 1), :] = jnp.sum(total, axis=0, keepdims=True)
    top[:width] = scale * lax.dot_general(feat_ref[0], grad_ref[...], NN, preferred_element_type=F32)
    top[width:] = scale * lax.dot_general(pairs[...].astype(BF), grad_ref[...], NN, preferred_element_type=F32)
    blocks, padded, lanes = keep_ref.shape
    rows = top.shape[0] // 2
    fill = jnp.zeros((padded - rows, lanes), F32)
    x, core = at_ref[0], at_ref[1]
    for b in range(blocks):
        column = pl.ds(pl.multiple_of((x + b) % blocks * lanes, lanes), lanes)
        halves = [jnp.concatenate([top[c * rows : (c + 1) * rows, column], fill], axis=0) for c in range(2)]
        keep_ref[b] = jnp.where(core == 0, halves[0], halves[1]).astype(BF)
        send_ref[b] = jnp.where(core == 0, halves[1], halves[0]).astype(BF)


def join_core_kernel(keep_ref, came_ref, *outs):
    for b, out in enumerate(outs):
        out[...] = (keep_ref[b].astype(F32) + came_ref[b].astype(F32)).astype(BF)


def total_of(refs):
    total = refs[0][...].astype(F32)
    for ref in refs[1:]:
        total += ref[...].astype(F32)
    return total


def join_x_kernel(at_ref, a, b, c, d, o0, o1, o2, o3, total):
    total[...] = total_of((a, b, c, d))
    rows = o0.shape[0]
    for n, out in enumerate((o0, o1, o2, o3)):
        begin = pl.multiple_of((at_ref[2] + n) % 4 * rows, rows)
        out[...] = total[pl.ds(begin, rows), :].astype(BF)


def join_y_kernel(a, b, c, d, out):
    total = total_of((a, b, c, d))
    fill = jnp.zeros((out.shape[0] - total.shape[0], total.shape[1]), F32)
    out[...] = jnp.concatenate([total, fill], axis=0).astype(BF)


def assemble_kernel(at_ref, a, b, c, d, other_ref, out, wide):
    x, core = at_ref[0], at_ref[1]
    rows = out.shape[0] // 2
    for n, mine in enumerate((a, b, c, d)):
        own, other = mine[...].astype(F32), other_ref[n].astype(F32)
        low = jnp.where(core == 0, own, other)[:rows]
        high = jnp.where(core == 0, other, own)[:rows]
        column = pl.ds(pl.multiple_of((x + 4 - n) % 4 * LANES, LANES), LANES)
        wide[:, column] = jnp.concatenate([low, high], axis=0)
    out[...] = wide[...].astype(BF)


def digits_kernel(order_ref, first_ref, last_ref, sorted_ref):
    order = order_ref[...]
    both = first_ref[...] * I3 + last_ref[...]
    row, lane = order // LANES, order % LANES
    total = jnp.zeros(order.shape, jnp.int32)
    for r in range(order.shape[0]):
        spread = jnp.broadcast_to(both[r : r + 1], order.shape)
        total = jnp.where(row == r, jnp.take_along_axis(spread, lane, axis=1), total)
    sorted_ref[...] = total


def onehot(digit, slots):
    lanes = digit.shape[1]
    return jnp.where(lax.broadcasted_iota(jnp.int32, (slots, lanes), 0) == digit, 1.0, 0.0).astype(BF)


def digits_of(sorted_ref, group, k):
    rows = group // LANES
    at = sorted_ref[pl.ds(k * rows, rows), :]
    at = jnp.concatenate([at[r : r + 1] for r in range(rows)], axis=1)
    return at // I3, at % I3


def before_kernel(sorted_ref, one_ref, mid_ref, three_ref, left_ref, right_ref, chained_ref):
    group = left_ref.shape[1]
    first, third = digits_of(sorted_ref, group, pl.program_id(0))
    left = lax.dot_general(one_ref[...], onehot(first, I1), NN, preferred_element_type=F32).astype(BF)
    left_ref[...] = left
    right_ref[...] = lax.dot_general(three_ref[...], onehot(third, I3), NN, preferred_element_type=F32).astype(BF)
    for a in range(D1):
        chained = lax.dot_general(mid_ref[0], left[a * R : (a + 1) * R], TN, preferred_element_type=F32)
        chained_ref[a * D2 * R : (a + 1) * D2 * R] = chained.astype(BF)


def place(r):
    return r % 2 * 8 + r // 4 * 2 + r // 2 % 2


def after_kernel(
    scale, start, reps, order_ref, sorted_ref, received_ref, left_ref, right_ref, chained_ref, mid_ref, *refs
):
    last = reps > 0
    if start:
        old_one_ref, old_three_ref, unused = refs[:3]
        refs = refs[3:]
    two_ref, *ends = refs[: 2 if last else 3]
    wide, picked, gt, inner, back, acc_one, acc_three, right_wide, chained_wide = refs[2 if last else 3 :]
    k = pl.program_id(0)
    groups = pl.num_programs(0)
    group = left_ref.shape[1]
    steps = (R // SUB) * (group // LANES)
    share = group // steps

    def fetch(slot, base, begin, number):
        for n in range(number):
            picked[slot, pl.ds(begin + n, 1), :] = wide[pl.ds(order_ref[base + begin + n], 1), :]

    @pl.when(k == 0)
    def _():
        wide[...] = received_ref[...].astype(F32)
        acc_one[...] = old_one_ref[...] if start else jnp.zeros_like(acc_one)
        acc_three[...] = old_three_ref[...] if start else jnp.zeros_like(acc_three)

        def one(step, carry):
            fetch(0, start * group, step * share, share)
            return carry

        lax.fori_loop(0, steps, one, 0)

    slot = k % 2
    later = (start + jnp.minimum(k + 1, groups - 1)) * group
    gt[...] = picked[slot].T
    right_wide[...] = right_ref[...].astype(F32)
    chained_wide[...] = chained_ref[...].astype(F32)

    def chunk(step, carry):
        fetch(1 - slot, later, step * share, share)
        half = step // (R // SUB)
        lanes = pl.ds(pl.multiple_of(half * LANES, LANES), LANES)
        low = (step % (R // SUB)) * SUB
        rights = [right_wide[pl.ds(pl.multiple_of(c * R + low, SUB), SUB), lanes] for c in range(D3)]
        totals = [None] * D3
        for j in range(D1 * D2):
            at = pl.ds(pl.multiple_of(j * R + low, SUB), SUB)
            link = chained_wide[at, lanes]
            total = None
            for c in range(D3):
                g = jnp.broadcast_to(gt[pl.ds(j * D3 + c, 1), lanes], (SUB, LANES))
                term = g * rights[c]
                total = term if total is None else total + term
                term = g * link
                totals[c] = term if totals[c] is None else totals[c] + term
            inner[at, lanes] = total
        for c in range(D3):
            back[pl.ds(pl.multiple_of(c * R + low, SUB), SUB), lanes] = totals[c]
        return carry

    lax.fori_loop(0, steps, chunk, 0)
    first, third = digits_of(sorted_ref, group, start + k)
    inner_all = inner[...].astype(BF)
    two = None
    firsts = []
    for a in range(D1):
        part = inner_all[a * D2 * R : (a + 1) * D2 * R]
        term = lax.dot_general(left_ref[a * R : (a + 1) * R], part, NT, preferred_element_type=F32)
        two = term if two is None else two + term
        firsts.append(lax.dot_general(mid_ref[0], part, NN, preferred_element_type=F32).astype(BF))
    two = (scale * two).astype(BF)
    for b in range(D2 * R // LANES):
        two_ref[0, b * R : (b + 1) * R] = two[:, b * LANES : (b + 1) * LANES]
    back_first = jnp.concatenate(firsts, axis=0)
    acc_one[...] += lax.dot_general(onehot(first, I1), back_first, NT, preferred_element_type=F32)
    acc_three[...] += lax.dot_general(onehot(third, I3), back[...].astype(BF), NT, preferred_element_type=F32)

    @pl.when(k == groups - 1)
    def _():
        if not last:
            ends[0][...] = acc_one[...]
            ends[1][...] = acc_three[...]
            return
        rest_ref = ends[0]
        for r in range(reps):
            blocks = []
            for acc in (acc_one, acc_three):
                rows = acc.shape[0] // reps
                for b in range(acc.shape[1] // LANES):
                    blocks.append(acc[r * rows : (r + 1) * rows, b * LANES : (b + 1) * LANES])
            rest_ref[place(r)] = (scale * jnp.concatenate(blocks, axis=0)).astype(BF)


SMEM = pl.BlockSpec(memory_space=pltpu.SMEM)
VMEM = pl.BlockSpec(memory_space=pltpu.VMEM)


def whole(shape):
    return pl.BlockSpec(shape, lambda *a: (0,) * len(shape))


def dense(bottom_out, pooled, top_grad, top_weight):
    samples, width = bottom_out.shape
    tables = pooled.shape[1]
    count = tables + 1
    return pl.pallas_call(
        lambda *refs: dense_kernel(count, *refs),
        out_shape=(
            jax.ShapeDtypeStruct((tables, samples, width), BF),
            jax.ShapeDtypeStruct((samples, width), BF),
            jax.ShapeDtypeStruct((count, width, samples), BF),
        ),
        scratch_shapes=[
            pltpu.VMEM((samples * tables, width), F32),
            pltpu.VMEM((count, width, samples), F32),
            pltpu.VMEM((top_weight.shape[0], samples), F32),
            pltpu.VMEM((count, width, samples), F32),
        ],
        compiler_params=pltpu.CompilerParams(vmem_limit_bytes=48 << 20),
        name="dense",
    )(bottom_out, pooled.reshape(samples * tables, width), top_grad, top_weight)


def gram(where, feat, top_grad, scale, shape):
    count, width, samples = feat.shape
    pairs = count * (count - 1) // 2
    return pl.pallas_call(
        lambda *refs: gram_kernel(count, scale, *refs),
        in_specs=[SMEM, VMEM, VMEM],
        out_shape=(jax.ShapeDtypeStruct(shape, BF),) * 2,
        scratch_shapes=[
            pltpu.VMEM((count, width, samples), F32),
            pltpu.VMEM((pairs, samples), F32),
            pltpu.VMEM((width + pairs, top_grad.shape[1]), F32),
        ],
        compiler_params=pltpu.CompilerParams(vmem_limit_bytes=48 << 20),
        name="gram",
    )(where, feat, top_grad)


def join_core(keep, came):
    return pl.pallas_call(
        join_core_kernel, out_shape=(jax.ShapeDtypeStruct(keep.shape[1:], BF),) * 4, name="join_core"
    )(keep, came)


def join_x(where, *parts):
    rows, lanes = parts[0].shape
    return pl.pallas_call(
        join_x_kernel,
        in_specs=[SMEM] + [VMEM] * 4,
        out_shape=(jax.ShapeDtypeStruct((rows // 4, lanes), BF),) * 4,
        scratch_shapes=[pltpu.VMEM((rows, lanes), F32)],
        name="join_x",
    )(where, *parts)


def join_y(*parts):
    return pl.pallas_call(
        join_y_kernel, out_shape=jax.ShapeDtypeStruct((LANES, LANES), BF), name="join_y"
    )(*parts)


def assemble(where, shape, *parts):
    return pl.pallas_call(
        assemble_kernel,
        in_specs=[SMEM] + [VMEM] * 5,
        out_shape=jax.ShapeDtypeStruct(shape, BF),
        scratch_shapes=[pltpu.VMEM(shape, F32)],
        name="assemble",
    )(where, *parts)


def before(order, first, last, core_one, core_two, core_three):
    total = order.shape[0]
    group = total // I2
    table = (total // LANES, LANES)
    sorted_digits = pl.pallas_call(
        digits_kernel, out_shape=jax.ShapeDtypeStruct(table, jnp.int32), name="digits"
    )(order.reshape(table), first.reshape(table), last.reshape(table))
    links = pl.pallas_call(
        before_kernel,
        grid=(I2,),
        in_specs=[
            whole(table),
            whole((D1 * R, I1)),
            pl.BlockSpec((1, R, D2 * R), lambda k: (k, 0, 0)),
            whole((D3 * R, I3)),
        ],
        out_specs=(
            pl.BlockSpec((D1 * R, group), lambda k: (0, k)),
            pl.BlockSpec((D3 * R, group), lambda k: (0, k)),
            pl.BlockSpec((D1 * D2 * R, group), lambda k: (0, k)),
        ),
        out_shape=(
            jax.ShapeDtypeStruct((D1 * R, total), BF),
            jax.ShapeDtypeStruct((D3 * R, total), BF),
            jax.ShapeDtypeStruct((D1 * D2 * R, total), BF),
        ),
        compiler_params=pltpu.CompilerParams(vmem_limit_bytes=48 << 20),
        name="before",
    )(sorted_digits, core_one.T, core_two, core_three.T)
    return sorted_digits, links


def after(begin, end, received, order, sorted_digits, links, core_two, scale, reps, old):
    rest = (I1 * D1 * R + I3 * D3 * R) // reps // LANES
    total, width = received.shape
    group = total // I2
    left, right, chained = links
    last = end == I2
    sums = (I1, D1 * R), (I3, D3 * R)
    two_shape = I2, R * D2 * R // LANES, LANES
    extra_in = [whole(sums[0]), whole(sums[1]), pl.BlockSpec(memory_space=pl.ANY)] if begin else []
    ends = [((reps, rest, LANES), BF)] if last else [(one, F32) for one in sums]
    return pl.pallas_call(
        lambda *refs: after_kernel(scale, begin, reps if last else 0, *refs),
        grid_spec=pltpu.PrefetchScalarGridSpec(
            num_scalar_prefetch=1,
            grid=(end - begin,),
            in_specs=[
                whole(sorted_digits.shape),
                whole((total, width)),
                pl.BlockSpec((D1 * R, group), lambda k, o: (0, begin + k)),
                pl.BlockSpec((D3 * R, group), lambda k, o: (0, begin + k)),
                pl.BlockSpec((D1 * D2 * R, group), lambda k, o: (0, begin + k)),
                pl.BlockSpec((1, R, D2 * R), lambda k, o: (begin + k, 0, 0)),
            ]
            + extra_in,
            out_specs=[
                pl.BlockSpec((1,) + two_shape[1:], lambda k, o: (place(begin + k), 0, 0)),
            ]
            + [whole(shape) for shape, kind in ends],
            scratch_shapes=[
                pltpu.VMEM((total, width), F32),
                pltpu.VMEM((2, group, width), F32),
                pltpu.VMEM((width, group), F32),
                pltpu.VMEM((D1 * D2 * R, group), F32),
                pltpu.VMEM((D3 * R, group), F32),
                pltpu.VMEM((I1, D1 * R), F32),
                pltpu.VMEM((I3, D3 * R), F32),
                pltpu.VMEM((D3 * R, group), F32),
                pltpu.VMEM((D1 * D2 * R, group), F32),
            ],
        ),
        out_shape=[jax.ShapeDtypeStruct(two_shape, BF)] + [jax.ShapeDtypeStruct(*one) for one in ends],
        input_output_aliases={9: 0} if begin else {},
        compiler_params=pltpu.CompilerParams(vmem_limit_bytes=48 << 20),
        name="after",
    )(order, sorted_digits, received, left, right, chained, core_two, *old)


CUTS = 5, 10
AXES = {"x": 4, "z_hi": 2, "core": 2, "y": 4, "z_lo": 8}


def groups_of(*names):
    places = np.arange(int(np.prod(list(AXES.values())))).reshape(tuple(AXES.values()))
    order = list(AXES)
    moved = [order.index(n) for n in names]
    kept = [i for i in range(len(order)) if i not in moved]
    return places.transpose(kept + moved).reshape(-1, int(np.prod([AXES[n] for n in names]))).tolist()


def swap(array, *names):
    return lax.all_to_all(
        array, ("rep", "tab"), 0, 0, axis_index_groups=groups_of(*names), tiled=True
    )


def add_up(array, *names):
    return jnp.sum(swap(array, *names).astype(F32), axis=0)


def shift(array, axis, by):
    size = 4
    step = 4 if axis == "rep" else 8
    number = size * step
    return lax.ppermute(array, axis, [(i, (i + by * step) % number) for i in range(number)])


def swap_core(array):
    return lax.ppermute(array, "rep", [(i, i ^ 1) for i in range(16)])


def gather_up(array, size, *names):
    return swap(jnp.broadcast_to(array[None], (size,) + array.shape), *names)


def on_device(
    bottom_out,
    pooled,
    top_grad,
    top_weight,
    core_first,
    core_mid,
    core_last,
    digit_first,
    digit_last,
    grouped,
):
    samples, width = bottom_out.shape
    reps = lax.axis_size("rep")
    batch_all = samples * reps * lax.axis_size("tab")
    scale = float(np.float32(1.0 / np.sqrt(batch_all)))
    grad_rows, grad_bottom, feat = dense(bottom_out, pooled, top_grad, top_weight)
    received = lax.all_to_all(grad_rows, "tab", split_axis=0, concat_axis=0, tiled=True)
    rep, tab = lax.axis_index("rep"), lax.axis_index("tab")
    where = jnp.stack([rep >> 2, rep & 1, tab >> 3]).astype(jnp.int32)
    rows = top_weight.shape[0]
    padded = -(-rows // 2 // 64) * 64
    quarter = padded // 4
    keep, send = gram(where, feat, top_grad, scale, (4, padded, LANES))
    own, *others = join_core(keep, swap_core(send))
    order, own, others = lax.optimization_barrier((grouped[0, 0], own, others))
    sorted_digits, links = before(
        order, digit_first[0], digit_last[0], core_first[0], core_mid[0], core_last[0]
    )
    own, *others = join_x(where, own, *[shift(one, "rep", 1 + n) for n, one in enumerate(others)])
    partial = join_y(own, *[shift(one, "tab", 1 + n) for n, one in enumerate(others)])
    received = received.reshape(-1, width)
    links, partial = lax.optimization_barrier((links, partial))
    received, partial = lax.optimization_barrier((received, partial))

    def piece(begin, end, old):
        return after(begin, end, received, order, sorted_digits, links, core_mid[0], scale, reps, old)

    two, one, three = piece(0, CUTS[0], ())
    summed = add_up(partial.reshape(16, SUB, LANES), "z_hi", "z_lo").astype(BF)
    one, summed = lax.optimization_barrier((one, summed))
    two, one, three = piece(CUTS[0], CUTS[1], (one, three, two))
    summed = gather_up(summed, 16, "z_hi", "z_lo").reshape(LANES, LANES)[:quarter]
    one, summed = lax.optimization_barrier((one, summed))
    two, rest = piece(CUTS[1], I2, (one, three, two))
    summed = gather_up(summed, 4, "y").reshape(padded, LANES)
    rest, summed = lax.optimization_barrier((rest, summed))
    mine = [summed] + [shift(summed, "rep", n) for n in (1, 2, 3)]
    grad_top = assemble(where, (rows, top_grad.shape[1]), *mine, swap_core(jnp.stack(mine)))
    parts = jnp.concatenate([two, rest], axis=1)
    parts = add_up(parts.reshape(2, 8, -1, LANES), "core").astype(BF)
    parts = add_up(parts.reshape(4, 2, -1, LANES), "x").astype(BF)
    share = add_up(parts, "z_hi")
    size_two = R * D2 * R // LANES
    size_one = I1 // reps * D1 * R // LANES
    widths = D2 * R // LANES, D1 * R // LANES, D3 * R // LANES

    def lay(block, blocks):
        return block.reshape(blocks, -1, LANES).swapaxes(0, 1).reshape(1, -1, blocks * LANES)

    grad_two = lay(share[:size_two], widths[0])[:, None]
    grad_one = lay(share[size_two : size_two + size_one], widths[1])
    grad_three = lay(share[size_two + size_one :], widths[2])
    return (grad_one, grad_two, grad_three, grad_top, grad_bottom)


def solution(mesh):
    return jax.shard_map(
        on_device,
        mesh=mesh,
        in_specs=(
            P(("rep", "tab"), None),
            P(("rep", "tab"), None, None),
            P(("rep", "tab"), None),
            P(),
            P("tab", None, None),
            P("tab", None, None, None),
            P("tab", None, None),
            P("tab", "rep"),
            P("tab", "rep"),
            P("tab", "rep", None),
        ),
        out_specs=(
            P("tab", "rep", None),
            P("tab", "rep", None, None),
            P("tab", "rep", None),
            P(),
            P(("rep", "tab"), None),
        ),
        check_vma=False,
    )
```

```python
import jax
import jax.numpy as jnp
import numpy as np
from jax import lax
from jax.experimental import pallas as pl
from jax.experimental.pallas import tpu as pltpu
from jax.sharding import PartitionSpec as P

D1 = 4
D2 = 4
D3 = 8
R = 64
I1 = 128
I2 = 16
I3 = 128
LANES = 128
SUB = 8
BF = jnp.bfloat16
F32 = jnp.float32
NT = (((1,), (1,)), ((), ()))
TN = (((0,), (0,)), ((), ()))
NN = (((1,), (0,)), ((), ()))


def pair(i, j):
    low, high = min(i, j), max(i, j)
    return high * (high - 1) // 2 + low


def dense_kernel(count, bottom_ref, pooled_ref, grad_ref, weight_ref, rows_ref, gbottom_ref, feat_ref, wide, feat, gi, out):
    samples, width = bottom_ref.shape
    tables = count - 1
    gi[...] = lax.dot_general(weight_ref[...], grad_ref[...], NT, preferred_element_type=F32)
    wide[...] = pooled_ref[...].astype(F32)
    feat[0] = bottom_ref[...].astype(F32).T
    for t in range(tables):
        feat[1 + t] = wide[pl.ds(t, samples, stride=tables), :].T
    feat_ref[...] = feat[...].astype(BF)

    def chunk(step, carry):
        at = pl.ds(pl.multiple_of(step * SUB, SUB), SUB)
        parts = [feat[j, at, :] for j in range(count)]
        for i in range(count):
            total = None
            for j in range(count):
                if j != i:
                    row = gi[pl.ds(width + pair(i, j), 1), :]
                    term = jnp.broadcast_to(row, (SUB, samples)) * parts[j]
                    total = term if total is None else total + term
            out[i, at, :] = total
        return carry

    lax.fori_loop(0, width // SUB, chunk, 0)
    gbottom_ref[...] = (out[0] + gi[pl.ds(0, width), :]).T.astype(BF)
    for t in range(tables):
        rows_ref[t] = out[1 + t].T.astype(BF)


def gram_kernel(count, scale, at_ref, feat_ref, grad_ref, keep_ref, send_ref, feat, pairs, top):
    width, samples = feat_ref.shape[1:]
    feat[...] = feat_ref[...].astype(F32)
    for i0 in range(0, count, 4):
        for j0 in range(0, count, 8):
            todo = [(i, j) for i in range(i0, min(i0 + 4, count)) for j in range(j0, min(j0 + 8, count)) if j < i]
            if not todo:
                continue
            used = sorted({i for one in todo for i in one})

            def chunk(step, totals, todo=todo, used=used):
                at = pl.ds(pl.multiple_of(step * SUB, SUB), SUB)
                parts = {i: feat[i, at, :] for i in used}
                return tuple(total + parts[i] * parts[j] for total, (i, j) in zip(totals, todo))

            zero = jnp.zeros((SUB, samples), F32)
            totals = lax.fori_loop(0, width // SUB, chunk, (zero,) * len(todo), unroll=2)
            for total, (i, j) in zip(totals, todo):
                pairs[pl.ds(pair(i, j), 1), :] = jnp.sum(total, axis=0, keepdims=True)
    top[:width] = scale * lax.dot_general(feat_ref[0], grad_ref[...], NN, preferred_element_type=F32)
    top[width:] = scale * lax.dot_general(pairs[...].astype(BF), grad_ref[...], NN, preferred_element_type=F32)
    blocks, padded, lanes = keep_ref.shape
    rows = top.shape[0] // 2
    fill = jnp.zeros((padded - rows, lanes), F32)
    x, core = at_ref[0], at_ref[1]
    for b in range(blocks):
        column = pl.ds(pl.multiple_of((x + b) % blocks * lanes, lanes), lanes)
        halves = [jnp.concatenate([top[c * rows : (c + 1) * rows, column], fill], axis=0) for c in range(2)]
        keep_ref[b] = jnp.where(core == 0, halves[0], halves[1]).astype(BF)
        send_ref[b] = jnp.where(core == 0, halves[1], halves[0]).astype(BF)


def join_core_kernel(keep_ref, came_ref, *outs):
    for b, out in enumerate(outs):
        out[...] = (keep_ref[b].astype(F32) + came_ref[b].astype(F32)).astype(BF)


def total_of(refs):
    total = refs[0][...].astype(F32)
    for ref in refs[1:]:
        total += ref[...].astype(F32)
    return total


def join_x_kernel(at_ref, a, b, c, d, o0, o1, o2, o3, total):
    total[...] = total_of((a, b, c, d))
    rows = o0.shape[0]
    for n, out in enumerate((o0, o1, o2, o3)):
        begin = pl.multiple_of((at_ref[2] + n) % 4 * rows, rows)
        out[...] = total[pl.ds(begin, rows), :].astype(BF)


def join_y_kernel(a, b, c, d, out):
    out[...] = total_of((a, b, c, d)).astype(BF)


def assemble_kernel(at_ref, mine_ref, other_ref, out, wide):
    core = at_ref[1]
    rows = out.shape[0] // 2
    for n in range(mine_ref.shape[0]):
        own, other = mine_ref[n].astype(F32), other_ref[n].astype(F32)
        low = jnp.where(core == 0, own, other)[:rows]
        high = jnp.where(core == 0, other, own)[:rows]
        wide[:, n * LANES : (n + 1) * LANES] = jnp.concatenate([low, high], axis=0)
    out[...] = wide[...].astype(BF)


def digits_kernel(order_ref, first_ref, last_ref, sorted_ref):
    order = order_ref[...]
    both = first_ref[...] * I3 + last_ref[...]
    row, lane = order // LANES, order % LANES
    total = jnp.zeros(order.shape, jnp.int32)
    for r in range(order.shape[0]):
        spread = jnp.broadcast_to(both[r : r + 1], order.shape)
        total = jnp.where(row == r, jnp.take_along_axis(spread, lane, axis=1), total)
    sorted_ref[...] = total


def onehot(digit, slots):
    lanes = digit.shape[1]
    return jnp.where(lax.broadcasted_iota(jnp.int32, (slots, lanes), 0) == digit, 1.0, 0.0).astype(BF)


def digits_of(sorted_ref, group, k):
    rows = group // LANES
    at = sorted_ref[pl.ds(k * rows, rows), :]
    at = jnp.concatenate([at[r : r + 1] for r in range(rows)], axis=1)
    return at // I3, at % I3


def before_kernel(sorted_ref, one_ref, mid_ref, three_ref, left_ref, right_ref, chained_ref):
    group = left_ref.shape[1]
    first, third = digits_of(sorted_ref, group, pl.program_id(0))
    left = lax.dot_general(one_ref[...], onehot(first, I1), NN, preferred_element_type=F32).astype(BF)
    left_ref[...] = left
    right_ref[...] = lax.dot_general(three_ref[...], onehot(third, I3), NN, preferred_element_type=F32).astype(BF)
    for a in range(D1):
        chained = lax.dot_general(mid_ref[0], left[a * R : (a + 1) * R], TN, preferred_element_type=F32)
        chained_ref[a * D2 * R : (a + 1) * D2 * R] = chained.astype(BF)


def place(r):
    return r % 2 * 8 + r // 4 * 2 + r // 2 % 2


def after_kernel(
    scale, start, reps, order_ref, sorted_ref, received_ref, left_ref, right_ref, chained_ref, mid_ref, *refs
):
    last = reps > 0
    if start:
        old_one_ref, old_three_ref, unused = refs[:3]
        refs = refs[3:]
    two_ref, *ends = refs[: 2 if last else 3]
    wide, picked, gt, inner, back, acc_one, acc_three, right_wide, chained_wide = refs[2 if last else 3 :]
    k = pl.program_id(0)
    groups = pl.num_programs(0)
    group = left_ref.shape[1]
    steps = (R // SUB) * (group // LANES)
    share = group // steps

    def fetch(slot, base, begin, number):
        for n in range(number):
            picked[slot, pl.ds(begin + n, 1), :] = wide[pl.ds(order_ref[base + begin + n], 1), :]

    @pl.when(k == 0)
    def _():
        wide[...] = received_ref[...].astype(F32)
        acc_one[...] = old_one_ref[...] if start else jnp.zeros_like(acc_one)
        acc_three[...] = old_three_ref[...] if start else jnp.zeros_like(acc_three)

        def one(step, carry):
            fetch(0, start * group, step * share, share)
            return carry

        lax.fori_loop(0, steps, one, 0)

    slot = k % 2
    later = (start + jnp.minimum(k + 1, groups - 1)) * group
    gt[...] = picked[slot].T
    right_wide[...] = right_ref[...].astype(F32)
    chained_wide[...] = chained_ref[...].astype(F32)

    def chunk(step, carry):
        fetch(1 - slot, later, step * share, share)
        half = step // (R // SUB)
        lanes = pl.ds(pl.multiple_of(half * LANES, LANES), LANES)
        low = (step % (R // SUB)) * SUB
        rights = [right_wide[pl.ds(pl.multiple_of(c * R + low, SUB), SUB), lanes] for c in range(D3)]
        totals = [None] * D3
        for j in range(D1 * D2):
            at = pl.ds(pl.multiple_of(j * R + low, SUB), SUB)
            link = chained_wide[at, lanes]
            total = None
            for c in range(D3):
                g = jnp.broadcast_to(gt[pl.ds(j * D3 + c, 1), lanes], (SUB, LANES))
                term = g * rights[c]
                total = term if total is None else total + term
                term = g * link
                totals[c] = term if totals[c] is None else totals[c] + term
            inner[at, lanes] = total
        for c in range(D3):
            back[pl.ds(pl.multiple_of(c * R + low, SUB), SUB), lanes] = totals[c]
        return carry

    lax.fori_loop(0, steps, chunk, 0)
    first, third = digits_of(sorted_ref, group, start + k)
    inner_all = inner[...].astype(BF)
    two = None
    firsts = []
    for a in range(D1):
        part = inner_all[a * D2 * R : (a + 1) * D2 * R]
        term = lax.dot_general(left_ref[a * R : (a + 1) * R], part, NT, preferred_element_type=F32)
        two = term if two is None else two + term
        firsts.append(lax.dot_general(mid_ref[0], part, NN, preferred_element_type=F32).astype(BF))
    two = (scale * two).astype(BF)
    for b in range(D2 * R // LANES):
        two_ref[0, b * R : (b + 1) * R] = two[:, b * LANES : (b + 1) * LANES]
    back_first = jnp.concatenate(firsts, axis=0)
    acc_one[...] += lax.dot_general(onehot(first, I1), back_first, NT, preferred_element_type=F32)
    acc_three[...] += lax.dot_general(onehot(third, I3), back[...].astype(BF), NT, preferred_element_type=F32)

    @pl.when(k == groups - 1)
    def _():
        if not last:
            ends[0][...] = acc_one[...]
            ends[1][...] = acc_three[...]
            return
        rest_ref = ends[0]
        for r in range(reps):
            blocks = []
            for acc in (acc_one, acc_three):
                rows = acc.shape[0] // reps
                for b in range(acc.shape[1] // LANES):
                    blocks.append(acc[r * rows : (r + 1) * rows, b * LANES : (b + 1) * LANES])
            rest_ref[place(r)] = (scale * jnp.concatenate(blocks, axis=0)).astype(BF)


SMEM = pl.BlockSpec(memory_space=pltpu.SMEM)
VMEM = pl.BlockSpec(memory_space=pltpu.VMEM)


def whole(shape):
    return pl.BlockSpec(shape, lambda *a: (0,) * len(shape))


def dense(bottom_out, pooled, top_grad, top_weight):
    samples, width = bottom_out.shape
    tables = pooled.shape[1]
    count = tables + 1
    return pl.pallas_call(
        lambda *refs: dense_kernel(count, *refs),
        out_shape=(
            jax.ShapeDtypeStruct((tables, samples, width), BF),
            jax.ShapeDtypeStruct((samples, width), BF),
            jax.ShapeDtypeStruct((count, width, samples), BF),
        ),
        scratch_shapes=[
            pltpu.VMEM((samples * tables, width), F32),
            pltpu.VMEM((count, width, samples), F32),
            pltpu.VMEM((top_weight.shape[0], samples), F32),
            pltpu.VMEM((count, width, samples), F32),
        ],
        compiler_params=pltpu.CompilerParams(vmem_limit_bytes=48 << 20),
        name="dense",
    )(bottom_out, pooled.reshape(samples * tables, width), top_grad, top_weight)


def gram(where, feat, top_grad, scale, shape):
    count, width, samples = feat.shape
    pairs = count * (count - 1) // 2
    return pl.pallas_call(
        lambda *refs: gram_kernel(count, scale, *refs),
        in_specs=[SMEM, VMEM, VMEM],
        out_shape=(jax.ShapeDtypeStruct(shape, BF),) * 2,
        scratch_shapes=[
            pltpu.VMEM((count, width, samples), F32),
            pltpu.VMEM((pairs, samples), F32),
            pltpu.VMEM((width + pairs, top_grad.shape[1]), F32),
        ],
        compiler_params=pltpu.CompilerParams(vmem_limit_bytes=48 << 20),
        name="gram",
    )(where, feat, top_grad)


def join_core(keep, came):
    return pl.pallas_call(
        join_core_kernel, out_shape=(jax.ShapeDtypeStruct(keep.shape[1:], BF),) * 4, name="join_core"
    )(keep, came)


def join_x(where, *parts):
    rows, lanes = parts[0].shape
    return pl.pallas_call(
        join_x_kernel,
        in_specs=[SMEM] + [VMEM] * 4,
        out_shape=(jax.ShapeDtypeStruct((rows // 4, lanes), BF),) * 4,
        scratch_shapes=[pltpu.VMEM((rows, lanes), F32)],
        name="join_x",
    )(where, *parts)


def join_y(*parts):
    return pl.pallas_call(
        join_y_kernel, out_shape=jax.ShapeDtypeStruct(parts[0].shape, BF), name="join_y"
    )(*parts)


def assemble(where, shape, *parts):
    return pl.pallas_call(
        assemble_kernel,
        in_specs=[SMEM, VMEM, VMEM],
        out_shape=jax.ShapeDtypeStruct(shape, BF),
        scratch_shapes=[pltpu.VMEM(shape, F32)],
        name="assemble",
    )(where, *parts)


def before(order, first, last, core_one, core_two, core_three):
    total = order.shape[0]
    group = total // I2
    table = (total // LANES, LANES)
    sorted_digits = pl.pallas_call(
        digits_kernel, out_shape=jax.ShapeDtypeStruct(table, jnp.int32), name="digits"
    )(order.reshape(table), first.reshape(table), last.reshape(table))
    links = pl.pallas_call(
        before_kernel,
        grid=(I2,),
        in_specs=[
            whole(table),
            whole((D1 * R, I1)),
            pl.BlockSpec((1, R, D2 * R), lambda k: (k, 0, 0)),
            whole((D3 * R, I3)),
        ],
        out_specs=(
            pl.BlockSpec((D1 * R, group), lambda k: (0, k)),
            pl.BlockSpec((D3 * R, group), lambda k: (0, k)),
            pl.BlockSpec((D1 * D2 * R, group), lambda k: (0, k)),
        ),
        out_shape=(
            jax.ShapeDtypeStruct((D1 * R, total), BF),
            jax.ShapeDtypeStruct((D3 * R, total), BF),
            jax.ShapeDtypeStruct((D1 * D2 * R, total), BF),
        ),
        compiler_params=pltpu.CompilerParams(vmem_limit_bytes=48 << 20),
        name="before",
    )(sorted_digits, core_one.T, core_two, core_three.T)
    return sorted_digits, links


def after(begin, end, received, order, sorted_digits, links, core_two, scale, reps, old):
    rest = (I1 * D1 * R + I3 * D3 * R) // reps // LANES
    total, width = received.shape
    group = total // I2
    left, right, chained = links
    last = end == I2
    sums = (I1, D1 * R), (I3, D3 * R)
    two_shape = I2, R * D2 * R // LANES, LANES
    extra_in = [whole(sums[0]), whole(sums[1]), pl.BlockSpec(memory_space=pl.ANY)] if begin else []
    ends = [((reps, rest, LANES), BF)] if last else [(one, F32) for one in sums]
    return pl.pallas_call(
        lambda *refs: after_kernel(scale, begin, reps if last else 0, *refs),
        grid_spec=pltpu.PrefetchScalarGridSpec(
            num_scalar_prefetch=1,
            grid=(end - begin,),
            in_specs=[
                whole(sorted_digits.shape),
                whole((total, width)),
                pl.BlockSpec((D1 * R, group), lambda k, o: (0, begin + k)),
                pl.BlockSpec((D3 * R, group), lambda k, o: (0, begin + k)),
                pl.BlockSpec((D1 * D2 * R, group), lambda k, o: (0, begin + k)),
                pl.BlockSpec((1, R, D2 * R), lambda k, o: (begin + k, 0, 0)),
            ]
            + extra_in,
            out_specs=[
                pl.BlockSpec((1,) + two_shape[1:], lambda k, o: (place(begin + k), 0, 0)),
            ]
            + [whole(shape) for shape, kind in ends],
            scratch_shapes=[
                pltpu.VMEM((total, width), F32),
                pltpu.VMEM((2, group, width), F32),
                pltpu.VMEM((width, group), F32),
                pltpu.VMEM((D1 * D2 * R, group), F32),
                pltpu.VMEM((D3 * R, group), F32),
                pltpu.VMEM((I1, D1 * R), F32),
                pltpu.VMEM((I3, D3 * R), F32),
                pltpu.VMEM((D3 * R, group), F32),
                pltpu.VMEM((D1 * D2 * R, group), F32),
            ],
        ),
        out_shape=[jax.ShapeDtypeStruct(two_shape, BF)] + [jax.ShapeDtypeStruct(*one) for one in ends],
        input_output_aliases={9: 0} if begin else {},
        compiler_params=pltpu.CompilerParams(vmem_limit_bytes=48 << 20),
        name="after",
    )(order, sorted_digits, received, left, right, chained, core_two, *old)


CUT = 8
AXES = {"x": 4, "z_hi": 2, "core": 2, "y": 4, "z_lo": 8}


def groups_of(*names):
    places = np.arange(int(np.prod(list(AXES.values())))).reshape(tuple(AXES.values()))
    order = list(AXES)
    moved = [order.index(n) for n in names]
    kept = [i for i in range(len(order)) if i not in moved]
    return places.transpose(kept + moved).reshape(-1, int(np.prod([AXES[n] for n in names]))).tolist()


def swap(array, *names):
    return lax.all_to_all(
        array, ("rep", "tab"), 0, 0, axis_index_groups=groups_of(*names), tiled=True
    )


def add_up(array, *names):
    return jnp.sum(swap(array, *names).astype(F32), axis=0)


def shift(array, axis, by):
    size = 4
    step = 4 if axis == "rep" else 8
    number = size * step
    return lax.ppermute(array, axis, [(i, (i + by * step) % number) for i in range(number)])


def swap_core(array):
    return lax.ppermute(array, "rep", [(i, i ^ 1) for i in range(16)])


def gather_up(array, size, *names):
    return swap(jnp.broadcast_to(array[None], (size,) + array.shape), *names)


def on_device(
    bottom_out,
    pooled,
    top_grad,
    top_weight,
    core_first,
    core_mid,
    core_last,
    digit_first,
    digit_last,
    grouped,
):
    samples, width = bottom_out.shape
    reps = lax.axis_size("rep")
    batch_all = samples * reps * lax.axis_size("tab")
    scale = float(np.float32(1.0 / np.sqrt(batch_all)))
    grad_rows, grad_bottom, feat = dense(bottom_out, pooled, top_grad, top_weight)
    received = lax.all_to_all(grad_rows, "tab", split_axis=0, concat_axis=0, tiled=True)
    rep, tab = lax.axis_index("rep"), lax.axis_index("tab")
    where = jnp.stack([rep >> 2, rep & 1, tab >> 3]).astype(jnp.int32)
    rows = top_weight.shape[0]
    padded = -(-rows // 2 // 64) * 64
    quarter = padded // 4
    keep, send = gram(where, feat, top_grad, scale, (4, padded, LANES))
    own, *others = join_core(keep, swap_core(send))
    order, own, others = lax.optimization_barrier((grouped[0, 0], own, others))
    sorted_digits, links = before(
        order, digit_first[0], digit_last[0], core_first[0], core_mid[0], core_last[0]
    )
    own, *others = join_x(where, own, *[shift(one, "rep", 1 + n) for n, one in enumerate(others)])
    partial = join_y(own, *[shift(one, "tab", 1 + n) for n, one in enumerate(others)])
    received = received.reshape(-1, width)
    links, partial = lax.optimization_barrier((links, partial))
    received, partial = lax.optimization_barrier((received, partial))

    def piece(begin, end, old):
        return after(begin, end, received, order, sorted_digits, links, core_mid[0], scale, reps, old)

    two, one, three = piece(0, CUT, ())
    copies = gather_up(partial, 16, "z_hi", "z_lo")
    summed = jnp.sum(copies.astype(F32), axis=0).astype(BF)
    one, summed = lax.optimization_barrier((one, summed))
    two, rest = piece(CUT, I2, (one, three, two))
    mine = gather_up(summed, 16, "x", "y").reshape(4, padded, LANES)
    rest, mine = lax.optimization_barrier((rest, mine))
    parts = jnp.concatenate([two, rest], axis=1)
    parts = add_up(parts.reshape(2, 8, -1, LANES), "core").astype(BF)
    parts = add_up(parts.reshape(4, 2, -1, LANES), "x")
    other_z = lax.ppermute(
        lax.dynamic_index_in_dim(parts, 1 - (rep >> 1 & 1), 0, False).astype(BF),
        "rep",
        [(i, i ^ 2) for i in range(16)],
    )
    share = lax.dynamic_index_in_dim(parts, rep >> 1 & 1, 0, False) + other_z.astype(F32)
    grad_top = assemble(where, (rows, top_grad.shape[1]), mine, swap_core(mine))
    size_two = R * D2 * R // LANES
    size_one = I1 // reps * D1 * R // LANES
    widths = D2 * R // LANES, D1 * R // LANES, D3 * R // LANES

    def lay(block, blocks):
        return block.reshape(blocks, -1, LANES).swapaxes(0, 1).reshape(1, -1, blocks * LANES)

    grad_two = lay(share[:size_two], widths[0])[:, None]
    grad_one = lay(share[size_two : size_two + size_one], widths[1])
    grad_three = lay(share[size_two + size_one :], widths[2])
    return (grad_one, grad_two, grad_three, grad_top, grad_bottom)


def solution(mesh):
    return jax.shard_map(
        on_device,
        mesh=mesh,
        in_specs=(
            P(("rep", "tab"), None),
            P(("rep", "tab"), None, None),
            P(("rep", "tab"), None),
            P(),
            P("tab", None, None),
            P("tab", None, None, None),
            P("tab", None, None),
            P("tab", "rep"),
            P("tab", "rep"),
            P("tab", "rep", None),
        ),
        out_specs=(
            P("tab", "rep", None),
            P("tab", "rep", None, None),
            P("tab", "rep", None),
            P(),
            P(("rep", "tab"), None),
        ),
        check_vma=False,
    )
```

```python
import jax
import jax.numpy as jnp
import numpy as np
from jax import lax
from jax.experimental import pallas as pl
from jax.experimental.pallas import tpu as pltpu
from jax.sharding import PartitionSpec as P

D1 = 4
D2 = 4
D3 = 8
R = 64
I1 = 128
I2 = 16
I3 = 128
LANES = 128
SUB = 8
TALL = 16
BF = jnp.bfloat16
F32 = jnp.float32
NT = (((1,), (1,)), ((), ()))
TN = (((0,), (0,)), ((), ()))
NN = (((1,), (0,)), ((), ()))


def pair(i, j):
    low, high = min(i, j), max(i, j)
    return high * (high - 1) // 2 + low


def dense_kernel(count, bottom_ref, pooled_ref, grad_ref, weight_ref, rows_ref, gbottom_ref, feat_ref, wide, feat, gi, out):
    samples, width = bottom_ref.shape
    tables = count - 1
    gi[...] = lax.dot_general(weight_ref[...], grad_ref[...], NT, preferred_element_type=F32)
    wide[...] = pooled_ref[...].astype(F32)
    feat[0] = bottom_ref[...].astype(F32).T
    for t in range(tables):
        feat[1 + t] = wide[pl.ds(t, samples, stride=tables), :].T
    feat_ref[...] = feat[...].astype(BF)

    def chunk(step, carry):
        at = pl.ds(pl.multiple_of(step * SUB, SUB), SUB)
        parts = [feat[j, at, :] for j in range(count)]
        for i in range(count):
            total = None
            for j in range(count):
                if j != i:
                    row = gi[pl.ds(width + pair(i, j), 1), :]
                    term = jnp.broadcast_to(row, (SUB, samples)) * parts[j]
                    total = term if total is None else total + term
            out[i, at, :] = total
        return carry

    lax.fori_loop(0, width // SUB, chunk, 0)
    gbottom_ref[...] = (out[0] + gi[pl.ds(0, width), :]).T.astype(BF)
    for t in range(tables):
        rows_ref[t] = out[1 + t].T.astype(BF)


def gram_kernel(count, scale, at_ref, feat_ref, grad_ref, keep_ref, send_ref, feat, pairs, top):
    width, samples = feat_ref.shape[1:]
    feat[...] = feat_ref[...].astype(F32)
    for i0 in range(0, count, 4):
        for j0 in range(0, count, 8):
            todo = [(i, j) for i in range(i0, min(i0 + 4, count)) for j in range(j0, min(j0 + 8, count)) if j < i]
            if not todo:
                continue
            used = sorted({i for one in todo for i in one})

            def chunk(step, totals, todo=todo, used=used):
                at = pl.ds(pl.multiple_of(step * SUB, SUB), SUB)
                parts = {i: feat[i, at, :] for i in used}
                return tuple(total + parts[i] * parts[j] for total, (i, j) in zip(totals, todo))

            zero = jnp.zeros((SUB, samples), F32)
            totals = lax.fori_loop(0, width // SUB, chunk, (zero,) * len(todo), unroll=2)
            for total, (i, j) in zip(totals, todo):
                pairs[pl.ds(pair(i, j), 1), :] = jnp.sum(total, axis=0, keepdims=True)
    top[:width] = scale * lax.dot_general(feat_ref[0], grad_ref[...], NN, preferred_element_type=F32)
    top[width:] = scale * lax.dot_general(pairs[...].astype(BF), grad_ref[...], NN, preferred_element_type=F32)
    blocks, padded, lanes = keep_ref.shape
    rows = top.shape[0] // 2
    fill = jnp.zeros((padded - rows, lanes), F32)
    x, core = at_ref[0], at_ref[1]
    for b in range(blocks):
        column = pl.ds(pl.multiple_of((x + b) % blocks * lanes, lanes), lanes)
        halves = [jnp.concatenate([top[c * rows : (c + 1) * rows, column], fill], axis=0) for c in range(2)]
        keep_ref[b] = jnp.where(core == 0, halves[0], halves[1]).astype(BF)
        send_ref[b] = jnp.where(core == 0, halves[1], halves[0]).astype(BF)


def join_core_kernel(keep_ref, came_ref, *outs):
    for b, out in enumerate(outs):
        out[...] = (keep_ref[b].astype(F32) + came_ref[b].astype(F32)).astype(BF)


def total_of(refs):
    total = refs[0][...].astype(F32)
    for ref in refs[1:]:
        total += ref[...].astype(F32)
    return total


def join_x_kernel(at_ref, a, b, c, d, o0, o1, o2, o3, total):
    total[...] = total_of((a, b, c, d))
    rows = o0.shape[0]
    for n, out in enumerate((o0, o1, o2, o3)):
        begin = pl.multiple_of((at_ref[2] + n) % 4 * rows, rows)
        out[...] = total[pl.ds(begin, rows), :].astype(BF)


def join_y_kernel(a, b, c, d, out):
    out[...] = jnp.broadcast_to(total_of((a, b, c, d)).astype(BF)[None], out.shape)


def join_z_kernel(copies_ref, out):
    total = copies_ref[0].astype(F32)
    for n in range(1, copies_ref.shape[0]):
        total += copies_ref[n].astype(F32)
    out[...] = jnp.broadcast_to(total.astype(BF)[None], out.shape)


def last_kernel(at_ref, parts_ref, other_ref, one_ref, two_ref, three_ref):
    own = jnp.where(at_ref[3] == 0, parts_ref[0], parts_ref[1])
    share = own + other_ref[...].astype(F32)
    begin = 0
    for out in (two_ref, one_ref, three_ref):
        rows = out.shape[0]
        for b in range(out.shape[1] // LANES):
            out[:, b * LANES : (b + 1) * LANES] = share[begin : begin + rows]
            begin += rows


def assemble_kernel(at_ref, mine_ref, other_ref, out, wide):
    core = at_ref[1]
    rows = out.shape[0] // 2
    for n in range(mine_ref.shape[0]):
        own, other = mine_ref[n].astype(F32), other_ref[n].astype(F32)
        low = jnp.where(core == 0, own, other)[:rows]
        high = jnp.where(core == 0, other, own)[:rows]
        wide[:, n * LANES : (n + 1) * LANES] = jnp.concatenate([low, high], axis=0)
    out[...] = wide[...].astype(BF)


def digits_kernel(order_ref, first_ref, last_ref, sorted_ref):
    order = order_ref[...]
    both = first_ref[...] * I3 + last_ref[...]
    row, lane = order // LANES, order % LANES
    total = jnp.zeros(order.shape, jnp.int32)
    for r in range(order.shape[0]):
        spread = jnp.broadcast_to(both[r : r + 1], order.shape)
        total = jnp.where(row == r, jnp.take_along_axis(spread, lane, axis=1), total)
    sorted_ref[...] = total


def onehot(digit, slots):
    lanes = digit.shape[1]
    return jnp.where(lax.broadcasted_iota(jnp.int32, (slots, lanes), 0) == digit, 1.0, 0.0).astype(BF)


def digits_of(sorted_ref, group, k):
    rows = group // LANES
    at = sorted_ref[pl.ds(k * rows, rows), :]
    at = jnp.concatenate([at[r : r + 1] for r in range(rows)], axis=1)
    return at // I3, at % I3


def before_kernel(sorted_ref, one_ref, mid_ref, three_ref, left_ref, right_ref, chained_ref):
    group = left_ref.shape[1]
    first, third = digits_of(sorted_ref, group, pl.program_id(0))
    left = lax.dot_general(one_ref[...], onehot(first, I1), NN, preferred_element_type=F32).astype(BF)
    left_ref[...] = left
    right_ref[...] = lax.dot_general(three_ref[...], onehot(third, I3), NN, preferred_element_type=F32).astype(BF)
    for a in range(D1):
        chained = lax.dot_general(mid_ref[0], left[a * R : (a + 1) * R], TN, preferred_element_type=F32)
        chained_ref[a * D2 * R : (a + 1) * D2 * R] = chained.astype(BF)


def place(r):
    return r % 2 * 8 + r // 4 * 2 + r // 2 % 2


def after_kernel(
    scale, start, reps, order_ref, sorted_ref, received_ref, left_ref, right_ref, chained_ref, mid_ref, *refs
):
    last = reps > 0
    if start:
        old_one_ref, old_three_ref, old_two_ref = refs[:3]
        refs = refs[3:]
    two_ref, *ends = refs[: 1 if last else 3]
    wide, picked, gt, inner, back, acc_one, acc_three = refs[1 if last else 3 :]
    k = pl.program_id(0)
    groups = pl.num_programs(0)
    group = left_ref.shape[1]
    steps = (R // TALL) * (group // LANES)
    share = group // steps

    def fetch(slot, base, begin, number):
        for n in range(number):
            picked[slot, pl.ds(begin + n, 1), :] = wide[pl.ds(order_ref[base + begin + n], 1), :]

    @pl.when(k == 0)
    def _():
        wide[...] = received_ref[...].astype(F32)
        acc_one[...] = old_one_ref[...] if start else jnp.zeros_like(acc_one)
        acc_three[...] = old_three_ref[...] if start else jnp.zeros_like(acc_three)

        for r in range(start):
            two_ref[place(r), : R * D2 * R // LANES] = old_two_ref[r]

        def one(step, carry):
            fetch(0, start * group, step * share, share)
            return carry

        lax.fori_loop(0, steps, one, 0)

    slot = k % 2
    later = (start + jnp.minimum(k + 1, groups - 1)) * group
    gt[...] = picked[slot].T

    def chunk(step, carry):
        fetch(1 - slot, later, step * share, share)
        lanes = pl.ds(pl.multiple_of(step // (R // TALL) * LANES, LANES), LANES)
        low = step % (R // TALL) * TALL
        rights = [right_ref[pl.ds(pl.multiple_of(c * R + low, TALL), TALL), lanes].astype(F32) for c in range(D3)]
        totals = [None] * D3
        for j in range(D1 * D2):
            at = pl.ds(pl.multiple_of(j * R + low, TALL), TALL)
            link = chained_ref[at, lanes].astype(F32)
            total = None
            for c in range(D3):
                g = jnp.broadcast_to(gt[pl.ds(j * D3 + c, 1), lanes], (TALL, LANES))
                term = g * rights[c]
                total = term if total is None else total + term
                term = g * link
                totals[c] = term if totals[c] is None else totals[c] + term
            inner[at, lanes] = total.astype(BF)
        for c in range(D3):
            back[pl.ds(pl.multiple_of(c * R + low, TALL), TALL), lanes] = totals[c].astype(BF)
        return carry

    lax.fori_loop(0, steps, chunk, 0)
    first, third = digits_of(sorted_ref, group, start + k)
    inner_all = inner[...]
    two = None
    firsts = []
    for a in range(D1):
        part = inner_all[a * D2 * R : (a + 1) * D2 * R]
        term = lax.dot_general(part, left_ref[a * R : (a + 1) * R], NT, preferred_element_type=F32)
        two = term if two is None else two + term
        firsts.append(lax.dot_general(mid_ref[0], part, NN, preferred_element_type=F32).astype(BF))
    two = (scale * two.T).astype(BF)
    into = place(start + k) if last else k
    for b in range(D2 * R // LANES):
        two_ref[into, b * R : (b + 1) * R] = two[:, b * LANES : (b + 1) * LANES]
    back_first = jnp.concatenate(firsts, axis=0)
    acc_one[...] += lax.dot_general(back_first, onehot(first, I1), NT, preferred_element_type=F32)
    acc_three[...] += lax.dot_general(back[...], onehot(third, I3), NT, preferred_element_type=F32)

    @pl.when(k == groups - 1)
    def _():
        if not last:
            ends[0][...] = acc_one[...]
            ends[1][...] = acc_three[...]
            return
        sums = acc_one[...].T, acc_three[...].T
        for r in range(reps):
            blocks = []
            for acc in sums:
                rows = acc.shape[0] // reps
                for b in range(acc.shape[1] // LANES):
                    blocks.append(acc[r * rows : (r + 1) * rows, b * LANES : (b + 1) * LANES])
            two_ref[place(r), R * D2 * R // LANES :] = (scale * jnp.concatenate(blocks, axis=0)).astype(BF)


SMEM = pl.BlockSpec(memory_space=pltpu.SMEM)
VMEM = pl.BlockSpec(memory_space=pltpu.VMEM)


def whole(shape):
    return pl.BlockSpec(shape, lambda *a: (0,) * len(shape))


def dense(bottom_out, pooled, top_grad, top_weight):
    samples, width = bottom_out.shape
    tables = pooled.shape[1]
    count = tables + 1
    return pl.pallas_call(
        lambda *refs: dense_kernel(count, *refs),
        out_shape=(
            jax.ShapeDtypeStruct((tables, samples, width), BF),
            jax.ShapeDtypeStruct((samples, width), BF),
            jax.ShapeDtypeStruct((count, width, samples), BF),
        ),
        scratch_shapes=[
            pltpu.VMEM((samples * tables, width), F32),
            pltpu.VMEM((count, width, samples), F32),
            pltpu.VMEM((top_weight.shape[0], samples), F32),
            pltpu.VMEM((count, width, samples), F32),
        ],
        compiler_params=pltpu.CompilerParams(vmem_limit_bytes=48 << 20),
        name="dense",
    )(bottom_out, pooled.reshape(samples * tables, width), top_grad, top_weight)


def gram(where, feat, top_grad, scale, shape):
    count, width, samples = feat.shape
    pairs = count * (count - 1) // 2
    return pl.pallas_call(
        lambda *refs: gram_kernel(count, scale, *refs),
        in_specs=[SMEM, VMEM, VMEM],
        out_shape=(jax.ShapeDtypeStruct(shape, BF),) * 2,
        scratch_shapes=[
            pltpu.VMEM((count, width, samples), F32),
            pltpu.VMEM((pairs, samples), F32),
            pltpu.VMEM((width + pairs, top_grad.shape[1]), F32),
        ],
        compiler_params=pltpu.CompilerParams(vmem_limit_bytes=48 << 20),
        name="gram",
    )(where, feat, top_grad)


def join_core(keep, came):
    return pl.pallas_call(
        join_core_kernel, out_shape=(jax.ShapeDtypeStruct(keep.shape[1:], BF),) * 4, name="join_core"
    )(keep, came)


def join_x(where, *parts):
    rows, lanes = parts[0].shape
    return pl.pallas_call(
        join_x_kernel,
        in_specs=[SMEM] + [VMEM] * 4,
        out_shape=(jax.ShapeDtypeStruct((rows // 4, lanes), BF),) * 4,
        scratch_shapes=[pltpu.VMEM((rows, lanes), F32)],
        name="join_x",
    )(where, *parts)


def join_y(*parts):
    return pl.pallas_call(
        join_y_kernel, out_shape=jax.ShapeDtypeStruct((16,) + parts[0].shape, BF), name="join_y"
    )(*parts)


def join_z(copies):
    return pl.pallas_call(
        join_z_kernel, out_shape=jax.ShapeDtypeStruct(copies.shape, BF), name="join_z"
    )(copies)


def last_sum(where, parts, other, reps):
    shapes = (I1 // reps, D1 * R), (R, D2 * R), (I3 // reps, D3 * R)
    return pl.pallas_call(
        last_kernel,
        in_specs=[SMEM, VMEM, VMEM],
        out_shape=[jax.ShapeDtypeStruct(shape, F32) for shape in shapes],
        name="last_sum",
    )(where, parts, other)


def assemble(where, shape, *parts):
    return pl.pallas_call(
        assemble_kernel,
        in_specs=[SMEM, VMEM, VMEM],
        out_shape=jax.ShapeDtypeStruct(shape, BF),
        scratch_shapes=[pltpu.VMEM(shape, F32)],
        name="assemble",
    )(where, *parts)


def before(order, first, last, core_one, core_two, core_three):
    total = order.shape[0]
    group = total // I2
    table = (total // LANES, LANES)
    sorted_digits = pl.pallas_call(
        digits_kernel, out_shape=jax.ShapeDtypeStruct(table, jnp.int32), name="digits"
    )(order.reshape(table), first.reshape(table), last.reshape(table))
    links = pl.pallas_call(
        before_kernel,
        grid=(I2,),
        in_specs=[
            whole(table),
            whole((D1 * R, I1)),
            pl.BlockSpec((1, R, D2 * R), lambda k: (k, 0, 0)),
            whole((D3 * R, I3)),
        ],
        out_specs=(
            pl.BlockSpec((D1 * R, group), lambda k: (0, k)),
            pl.BlockSpec((D3 * R, group), lambda k: (0, k)),
            pl.BlockSpec((D1 * D2 * R, group), lambda k: (0, k)),
        ),
        out_shape=(
            jax.ShapeDtypeStruct((D1 * R, total), BF),
            jax.ShapeDtypeStruct((D3 * R, total), BF),
            jax.ShapeDtypeStruct((D1 * D2 * R, total), BF),
        ),
        compiler_params=pltpu.CompilerParams(vmem_limit_bytes=48 << 20),
        name="before",
    )(sorted_digits, core_one.T, core_two, core_three.T)
    return sorted_digits, links


def after(begin, end, received, order, sorted_digits, links, core_two, scale, reps, old):
    rest = (I1 * D1 * R + I3 * D3 * R) // reps // LANES
    total, width = received.shape
    group = total // I2
    left, right, chained = links
    last = end == I2
    sums = (D1 * R, I1), (D3 * R, I3)
    size_two = R * D2 * R // LANES
    extra_in = [whole(sums[0]), whole(sums[1]), whole((begin, size_two, LANES))] if begin else []
    if last:
        outs = [((reps, size_two + rest, LANES), BF)]
    else:
        outs = [((end - begin, size_two, LANES), BF)] + [(one, F32) for one in sums]
    return pl.pallas_call(
        lambda *refs: after_kernel(scale, begin, reps if last else 0, *refs),
        grid_spec=pltpu.PrefetchScalarGridSpec(
            num_scalar_prefetch=1,
            grid=(end - begin,),
            in_specs=[
                whole(sorted_digits.shape),
                whole((total, width)),
                pl.BlockSpec((D1 * R, group), lambda k, o: (0, begin + k)),
                pl.BlockSpec((D3 * R, group), lambda k, o: (0, begin + k)),
                pl.BlockSpec((D1 * D2 * R, group), lambda k, o: (0, begin + k)),
                pl.BlockSpec((1, R, D2 * R), lambda k, o: (begin + k, 0, 0)),
            ]
            + extra_in,
            out_specs=[whole(shape) for shape, kind in outs],
            scratch_shapes=[
                pltpu.VMEM((total, width), F32),
                pltpu.VMEM((2, group, width), F32),
                pltpu.VMEM((width, group), F32),
                pltpu.VMEM((D1 * D2 * R, group), BF),
                pltpu.VMEM((D3 * R, group), BF),
                pltpu.VMEM((D1 * R, I1), F32),
                pltpu.VMEM((D3 * R, I3), F32),
            ],
        ),
        out_shape=[jax.ShapeDtypeStruct(*one) for one in outs],
        compiler_params=pltpu.CompilerParams(vmem_limit_bytes=48 << 20),
        name="after",
    )(order, sorted_digits, received, left, right, chained, core_two, *old)


CUT = 8
AXES = {"x": 4, "z_hi": 2, "core": 2, "y": 4, "z_lo": 8}


def groups_of(*names):
    places = np.arange(int(np.prod(list(AXES.values())))).reshape(tuple(AXES.values()))
    order = list(AXES)
    moved = [order.index(n) for n in names]
    kept = [i for i in range(len(order)) if i not in moved]
    return places.transpose(kept + moved).reshape(-1, int(np.prod([AXES[n] for n in names]))).tolist()


def swap(array, *names):
    return lax.all_to_all(
        array, ("rep", "tab"), 0, 0, axis_index_groups=groups_of(*names), tiled=True
    )


def add_up(array, *names):
    return jnp.sum(swap(array, *names).astype(F32), axis=0)


def shift(array, axis, by):
    size = 4
    step = 4 if axis == "rep" else 8
    number = size * step
    return lax.ppermute(array, axis, [(i, (i + by * step) % number) for i in range(number)])


def swap_core(array):
    return lax.ppermute(array, "rep", [(i, i ^ 1) for i in range(16)])


def gather_up(array, size, *names):
    return swap(jnp.broadcast_to(array[None], (size,) + array.shape), *names)


def on_device(
    bottom_out,
    pooled,
    top_grad,
    top_weight,
    core_first,
    core_mid,
    core_last,
    digit_first,
    digit_last,
    grouped,
):
    samples, width = bottom_out.shape
    reps = lax.axis_size("rep")
    batch_all = samples * reps * lax.axis_size("tab")
    scale = float(np.float32(1.0 / np.sqrt(batch_all)))
    grad_rows, grad_bottom, feat = dense(bottom_out, pooled, top_grad, top_weight)
    received = lax.all_to_all(grad_rows, "tab", split_axis=0, concat_axis=0, tiled=True)
    rep, tab = lax.axis_index("rep"), lax.axis_index("tab")
    where = jnp.stack([rep >> 2, rep & 1, tab >> 3, rep >> 1 & 1]).astype(jnp.int32)
    rows = top_weight.shape[0]
    padded = -(-rows // 2 // 64) * 64
    quarter = padded // 4
    keep, send = gram(where, feat, top_grad, scale, (4, padded, LANES))
    own, *others = join_core(keep, swap_core(send))
    order, own, others = lax.optimization_barrier((grouped[0, 0], own, others))
    sorted_digits, links = before(
        order, digit_first[0], digit_last[0], core_first[0], core_mid[0], core_last[0]
    )
    own, *others = join_x(where, own, *[shift(one, "rep", 1 + n) for n, one in enumerate(others)])
    partial = join_y(own, *[shift(one, "tab", 1 + n) for n, one in enumerate(others)])
    received = received.reshape(-1, width)
    links, partial = lax.optimization_barrier((links, partial))
    received, partial = lax.optimization_barrier((received, partial))

    def piece(begin, end, old):
        return after(begin, end, received, order, sorted_digits, links, core_mid[0], scale, reps, old)

    two, one, three = piece(0, CUT, ())
    summed = join_z(swap(partial, "z_hi", "z_lo"))
    one, summed = lax.optimization_barrier((one, summed))
    (parts,) = piece(CUT, I2, (one, three, two))
    mine = swap(summed, "x", "y").reshape(4, padded, LANES)
    parts, mine = lax.optimization_barrier((parts, mine))
    parts = add_up(parts.reshape(2, 8, -1, LANES), "core").astype(BF)
    parts = add_up(parts.reshape(4, 2, -1, LANES), "x")
    grad_top = assemble(where, (rows, top_grad.shape[1]), mine, swap_core(mine))
    parts, grad_top = lax.optimization_barrier((parts, grad_top))
    sent = jnp.where(where[3] == 0, parts[1], parts[0]).astype(BF)
    other = lax.ppermute(sent, "rep", [(i, i ^ 2) for i in range(16)])
    grad_one, grad_two, grad_three = last_sum(where, parts, other, reps)
    grad_one, grad_two, grad_three = grad_one[None], grad_two[None, None], grad_three[None]
    return (grad_one, grad_two, grad_three, grad_top, grad_bottom)


def solution(mesh):
    return jax.shard_map(
        on_device,
        mesh=mesh,
        in_specs=(
            P(("rep", "tab"), None),
            P(("rep", "tab"), None, None),
            P(("rep", "tab"), None),
            P(),
            P("tab", None, None),
            P("tab", None, None, None),
            P("tab", None, None),
            P("tab", "rep"),
            P("tab", "rep"),
            P("tab", "rep", None),
        ),
        out_specs=(
            P("tab", "rep", None),
            P("tab", "rep", None, None),
            P("tab", "rep", None),
            P(),
            P(("rep", "tab"), None),
        ),
        check_vma=False,
    )
```

```python
import jax
import jax.numpy as jnp
import numpy as np
from jax import lax
from jax.experimental import pallas as pl
from jax.experimental.pallas import tpu as pltpu
from jax.sharding import PartitionSpec as P

D1 = 4
D2 = 4
D3 = 8
R = 64
I1 = 128
I2 = 16
I3 = 128
LANES = 128
SUB = 8
TALL = 16
BF = jnp.bfloat16
F32 = jnp.float32
NT = (((1,), (1,)), ((), ()))
TN = (((0,), (0,)), ((), ()))
NN = (((1,), (0,)), ((), ()))


def pair(i, j):
    low, high = min(i, j), max(i, j)
    return high * (high - 1) // 2 + low


def dense_kernel(count, bottom_ref, pooled_ref, grad_ref, weight_ref, rows_ref, gbottom_ref, feat_ref, wide, feat, gi, out):
    samples, width = bottom_ref.shape
    tables = count - 1
    gi[...] = lax.dot_general(weight_ref[...], grad_ref[...], NT, preferred_element_type=F32)
    wide[...] = pooled_ref[...].astype(F32)
    feat[0] = bottom_ref[...].astype(F32).T
    for t in range(tables):
        feat[1 + t] = wide[pl.ds(t, samples, stride=tables), :].T
    feat_ref[...] = feat[...].astype(BF)

    def chunk(step, carry):
        at = pl.ds(pl.multiple_of(step * SUB, SUB), SUB)
        parts = [feat[j, at, :] for j in range(count)]
        for i in range(count):
            total = None
            for j in range(count):
                if j != i:
                    row = gi[pl.ds(width + pair(i, j), 1), :]
                    term = jnp.broadcast_to(row, (SUB, samples)) * parts[j]
                    total = term if total is None else total + term
            out[i, at, :] = total
        return carry

    lax.fori_loop(0, width // SUB, chunk, 0)
    gbottom_ref[...] = (out[0] + gi[pl.ds(0, width), :]).T.astype(BF)
    for t in range(tables):
        rows_ref[t] = out[1 + t].T.astype(BF)


def gram_kernel(count, scale, at_ref, feat_ref, grad_ref, keep_ref, send_ref, feat, pairs, top):
    width, samples = feat_ref.shape[1:]
    feat[...] = feat_ref[...].astype(F32)
    for i0 in range(0, count, 4):
        for j0 in range(0, count, 8):
            todo = [(i, j) for i in range(i0, min(i0 + 4, count)) for j in range(j0, min(j0 + 8, count)) if j < i]
            if not todo:
                continue
            used = sorted({i for one in todo for i in one})

            def chunk(step, totals, todo=todo, used=used):
                at = pl.ds(pl.multiple_of(step * SUB, SUB), SUB)
                parts = {i: feat[i, at, :] for i in used}
                return tuple(total + parts[i] * parts[j] for total, (i, j) in zip(totals, todo))

            zero = jnp.zeros((SUB, samples), F32)
            totals = lax.fori_loop(0, width // SUB, chunk, (zero,) * len(todo), unroll=2)
            for total, (i, j) in zip(totals, todo):
                pairs[pl.ds(pair(i, j), 1), :] = jnp.sum(total, axis=0, keepdims=True)
    top[:width] = scale * lax.dot_general(feat_ref[0], grad_ref[...], NN, preferred_element_type=F32)
    top[width:] = scale * lax.dot_general(pairs[...].astype(BF), grad_ref[...], NN, preferred_element_type=F32)
    blocks, padded, lanes = keep_ref.shape
    rows = top.shape[0] // 2
    fill = jnp.zeros((padded - rows, lanes), F32)
    x, core = at_ref[0], at_ref[1]
    for b in range(blocks):
        column = pl.ds(pl.multiple_of((x + b) % blocks * lanes, lanes), lanes)
        halves = [jnp.concatenate([top[c * rows : (c + 1) * rows, column], fill], axis=0) for c in range(2)]
        keep_ref[b] = jnp.where(core == 0, halves[0], halves[1]).astype(BF)
        send_ref[b] = jnp.where(core == 0, halves[1], halves[0]).astype(BF)


def join_core_kernel(keep_ref, came_ref, *outs):
    for b, out in enumerate(outs):
        out[...] = (keep_ref[b].astype(F32) + came_ref[b].astype(F32)).astype(BF)


def total_of(refs):
    total = refs[0][...].astype(F32)
    for ref in refs[1:]:
        total += ref[...].astype(F32)
    return total


def join_x_kernel(at_ref, a, b, c, d, o0, o1, o2, o3, total):
    total[...] = total_of((a, b, c, d))
    rows = o0.shape[0]
    for n, out in enumerate((o0, o1, o2, o3)):
        begin = pl.multiple_of((at_ref[2] + n) % 4 * rows, rows)
        out[...] = total[pl.ds(begin, rows), :].astype(BF)


def join_y_kernel(a, b, c, d, out):
    out[...] = jnp.broadcast_to(total_of((a, b, c, d)).astype(BF)[None], out.shape)


def join_z_kernel(copies_ref, out):
    total = copies_ref[0].astype(F32)
    for n in range(1, copies_ref.shape[0]):
        total += copies_ref[n].astype(F32)
    out[...] = jnp.broadcast_to(total.astype(BF)[None], out.shape)


def last_kernel(at_ref, parts_ref, other_ref, one_ref, two_ref, three_ref):
    own = jnp.where(at_ref[3] == 0, parts_ref[0], parts_ref[1])
    share = own + other_ref[...].astype(F32)
    begin = 0
    for out in (two_ref, one_ref, three_ref):
        rows = out.shape[0]
        for b in range(out.shape[1] // LANES):
            out[:, b * LANES : (b + 1) * LANES] = share[begin : begin + rows]
            begin += rows


def assemble_kernel(at_ref, mine_ref, other_ref, out, wide):
    core = at_ref[1]
    rows = out.shape[0] // 2
    for n in range(mine_ref.shape[0]):
        own, other = mine_ref[n].astype(F32), other_ref[n].astype(F32)
        low = jnp.where(core == 0, own, other)[:rows]
        high = jnp.where(core == 0, other, own)[:rows]
        wide[:, n * LANES : (n + 1) * LANES] = jnp.concatenate([low, high], axis=0)
    out[...] = wide[...].astype(BF)


def digits_kernel(order_ref, first_ref, last_ref, sorted_ref):
    order = order_ref[...]
    both = first_ref[...] * I3 + last_ref[...]
    row, lane = order // LANES, order % LANES
    total = jnp.zeros(order.shape, jnp.int32)
    for r in range(order.shape[0]):
        spread = jnp.broadcast_to(both[r : r + 1], order.shape)
        total = jnp.where(row == r, jnp.take_along_axis(spread, lane, axis=1), total)
    sorted_ref[...] = total


def onehot(digit, slots):
    lanes = digit.shape[1]
    return jnp.where(lax.broadcasted_iota(jnp.int32, (slots, lanes), 0) == digit, 1.0, 0.0).astype(BF)


def digits_of(sorted_ref, group, k):
    rows = group // LANES
    at = sorted_ref[pl.ds(k * rows, rows), :]
    at = jnp.concatenate([at[r : r + 1] for r in range(rows)], axis=1)
    return at // I3, at % I3


def before_kernel(sorted_ref, one_ref, mid_ref, three_ref, left_ref, right_ref, chained_ref):
    group = left_ref.shape[1]
    first, third = digits_of(sorted_ref, group, pl.program_id(0))
    left = lax.dot_general(one_ref[...], onehot(first, I1), NN, preferred_element_type=F32).astype(BF)
    left_ref[...] = left
    right_ref[...] = lax.dot_general(three_ref[...], onehot(third, I3), NN, preferred_element_type=F32).astype(BF)
    for a in range(D1):
        chained = lax.dot_general(mid_ref[0], left[a * R : (a + 1) * R], TN, preferred_element_type=F32)
        chained_ref[a * D2 * R : (a + 1) * D2 * R] = chained.astype(BF)


def place(r):
    return r % 2 * 8 + r // 4 * 2 + r // 2 % 2


def after_kernel(
    scale, start, reps, order_ref, sorted_ref, received_ref, left_ref, right_ref, chained_ref, mid_ref, *refs
):
    last = reps > 0
    if start:
        old_one_ref, old_three_ref, old_two_ref = refs[:3]
        refs = refs[3:]
    two_ref, *ends = refs[: 1 if last else 3]
    wide, picked, gt, inner, back, acc_one, acc_three = refs[1 if last else 3 :]
    k = pl.program_id(0)
    groups = pl.num_programs(0)
    group = left_ref.shape[1]
    steps = (R // TALL) * (group // LANES)
    share = group // steps

    def fetch(slot, base, begin, number):
        for n in range(number):
            picked[slot, pl.ds(begin + n, 1), :] = wide[pl.ds(order_ref[base + begin + n], 1), :]

    @pl.when(k == 0)
    def _():
        wide[...] = received_ref[...].astype(F32)
        acc_one[...] = old_one_ref[...] if start else jnp.zeros_like(acc_one)
        acc_three[...] = old_three_ref[...] if start else jnp.zeros_like(acc_three)

        for r in range(start):
            two_ref[place(r), : R * D2 * R // LANES] = old_two_ref[r]

        def one(step, carry):
            fetch(0, start * group, step * share, share)
            return carry

        lax.fori_loop(0, steps, one, 0)

    slot = k % 2
    later = (start + jnp.minimum(k + 1, groups - 1)) * group
    gt[...] = picked[slot].T

    def chunk(step, carry):
        fetch(1 - slot, later, step * share, share)
        lanes = pl.ds(pl.multiple_of(step // (R // TALL) * LANES, LANES), LANES)
        low = step % (R // TALL) * TALL
        rights = [right_ref[pl.ds(pl.multiple_of(c * R + low, TALL), TALL), lanes].astype(F32) for c in range(D3)]
        totals = [None] * D3
        for j in range(D1 * D2):
            at = pl.ds(pl.multiple_of(j * R + low, TALL), TALL)
            link = chained_ref[at, lanes].astype(F32)
            total = None
            for c in range(D3):
                g = jnp.broadcast_to(gt[pl.ds(j * D3 + c, 1), lanes], (TALL, LANES))
                term = g * rights[c]
                total = term if total is None else total + term
                term = g * link
                totals[c] = term if totals[c] is None else totals[c] + term
            inner[at, lanes] = total.astype(BF)
        for c in range(D3):
            back[pl.ds(pl.multiple_of(c * R + low, TALL), TALL), lanes] = totals[c].astype(BF)
        return carry

    lax.fori_loop(0, steps, chunk, 0)
    first, third = digits_of(sorted_ref, group, start + k)
    inner_all = inner[...]
    two = None
    firsts = []
    for a in range(D1):
        part = inner_all[a * D2 * R : (a + 1) * D2 * R]
        term = lax.dot_general(part, left_ref[a * R : (a + 1) * R], NT, preferred_element_type=F32)
        two = term if two is None else two + term
        firsts.append(lax.dot_general(mid_ref[0], part, NN, preferred_element_type=F32).astype(BF))
    two = (scale * two.T).astype(BF)
    into = place(start + k) if last else k
    for b in range(D2 * R // LANES):
        two_ref[into, b * R : (b + 1) * R] = two[:, b * LANES : (b + 1) * LANES]
    back_first = jnp.concatenate(firsts, axis=0)
    acc_one[...] += lax.dot_general(back_first, onehot(first, I1), NT, preferred_element_type=F32)
    acc_three[...] += lax.dot_general(back[...], onehot(third, I3), NT, preferred_element_type=F32)

    @pl.when(k == groups - 1)
    def _():
        if not last:
            ends[0][...] = acc_one[...]
            ends[1][...] = acc_three[...]
            return
        sums = acc_one[...].T, acc_three[...].T
        for r in range(reps):
            blocks = []
            for acc in sums:
                rows = acc.shape[0] // reps
                for b in range(acc.shape[1] // LANES):
                    blocks.append(acc[r * rows : (r + 1) * rows, b * LANES : (b + 1) * LANES])
            two_ref[place(r), R * D2 * R // LANES :] = (scale * jnp.concatenate(blocks, axis=0)).astype(BF)


SMEM = pl.BlockSpec(memory_space=pltpu.SMEM)
VMEM = pl.BlockSpec(memory_space=pltpu.VMEM)


def whole(shape):
    return pl.BlockSpec(shape, lambda *a: (0,) * len(shape))


def dense(bottom_out, pooled, top_grad, top_weight):
    samples, width = bottom_out.shape
    tables = pooled.shape[1]
    count = tables + 1
    return pl.pallas_call(
        lambda *refs: dense_kernel(count, *refs),
        out_shape=(
            jax.ShapeDtypeStruct((tables, samples, width), BF),
            jax.ShapeDtypeStruct((samples, width), BF),
            jax.ShapeDtypeStruct((count, width, samples), BF),
        ),
        scratch_shapes=[
            pltpu.VMEM((samples * tables, width), F32),
            pltpu.VMEM((count, width, samples), F32),
            pltpu.VMEM((top_weight.shape[0], samples), F32),
            pltpu.VMEM((count, width, samples), F32),
        ],
        compiler_params=pltpu.CompilerParams(vmem_limit_bytes=48 << 20),
        name="dense",
    )(bottom_out, pooled.reshape(samples * tables, width), top_grad, top_weight)


def gram(where, feat, top_grad, scale, shape):
    count, width, samples = feat.shape
    pairs = count * (count - 1) // 2
    return pl.pallas_call(
        lambda *refs: gram_kernel(count, scale, *refs),
        in_specs=[SMEM, VMEM, VMEM],
        out_shape=(jax.ShapeDtypeStruct(shape, BF),) * 2,
        scratch_shapes=[
            pltpu.VMEM((count, width, samples), F32),
            pltpu.VMEM((pairs, samples), F32),
            pltpu.VMEM((width + pairs, top_grad.shape[1]), F32),
        ],
        compiler_params=pltpu.CompilerParams(vmem_limit_bytes=48 << 20),
        name="gram",
    )(where, feat, top_grad)


def join_core(keep, came):
    return pl.pallas_call(
        join_core_kernel, out_shape=(jax.ShapeDtypeStruct(keep.shape[1:], BF),) * 4, name="join_core"
    )(keep, came)


def join_x(where, *parts):
    rows, lanes = parts[0].shape
    return pl.pallas_call(
        join_x_kernel,
        in_specs=[SMEM] + [VMEM] * 4,
        out_shape=(jax.ShapeDtypeStruct((rows // 4, lanes), BF),) * 4,
        scratch_shapes=[pltpu.VMEM((rows, lanes), F32)],
        name="join_x",
    )(where, *parts)


def join_y(*parts):
    return pl.pallas_call(
        join_y_kernel, out_shape=jax.ShapeDtypeStruct((16,) + parts[0].shape, BF), name="join_y"
    )(*parts)


def join_z(copies):
    return pl.pallas_call(
        join_z_kernel, out_shape=jax.ShapeDtypeStruct(copies.shape, BF), name="join_z"
    )(copies)


def last_sum(where, parts, other, reps):
    shapes = (I1 // reps, D1 * R), (R, D2 * R), (I3 // reps, D3 * R)
    return pl.pallas_call(
        last_kernel,
        in_specs=[SMEM, VMEM, VMEM],
        out_shape=[jax.ShapeDtypeStruct(shape, F32) for shape in shapes],
        name="last_sum",
    )(where, parts, other)


def assemble(where, shape, *parts):
    return pl.pallas_call(
        assemble_kernel,
        in_specs=[SMEM, VMEM, VMEM],
        out_shape=jax.ShapeDtypeStruct(shape, BF),
        scratch_shapes=[pltpu.VMEM(shape, F32)],
        name="assemble",
    )(where, *parts)


def before(order, first, last, core_one, core_two, core_three):
    total = order.shape[0]
    group = total // I2
    table = (total // LANES, LANES)
    sorted_digits = pl.pallas_call(
        digits_kernel, out_shape=jax.ShapeDtypeStruct(table, jnp.int32), name="digits"
    )(order.reshape(table), first.reshape(table), last.reshape(table))
    links = pl.pallas_call(
        before_kernel,
        grid=(I2,),
        in_specs=[
            whole(table),
            whole((D1 * R, I1)),
            pl.BlockSpec((1, R, D2 * R), lambda k: (k, 0, 0)),
            whole((D3 * R, I3)),
        ],
        out_specs=(
            pl.BlockSpec((D1 * R, group), lambda k: (0, k)),
            pl.BlockSpec((D3 * R, group), lambda k: (0, k)),
            pl.BlockSpec((D1 * D2 * R, group), lambda k: (0, k)),
        ),
        out_shape=(
            jax.ShapeDtypeStruct((D1 * R, total), BF),
            jax.ShapeDtypeStruct((D3 * R, total), BF),
            jax.ShapeDtypeStruct((D1 * D2 * R, total), BF),
        ),
        compiler_params=pltpu.CompilerParams(vmem_limit_bytes=48 << 20),
        name="before",
    )(sorted_digits, core_one.T, core_two, core_three.T)
    return sorted_digits, links


def after(begin, end, received, order, sorted_digits, links, core_two, scale, reps, old):
    rest = (I1 * D1 * R + I3 * D3 * R) // reps // LANES
    total, width = received.shape
    group = total // I2
    left, right, chained = links
    last = end == I2
    sums = (D1 * R, I1), (D3 * R, I3)
    size_two = R * D2 * R // LANES
    extra_in = [whole(sums[0]), whole(sums[1]), whole((begin, size_two, LANES))] if begin else []
    if last:
        outs = [((reps, size_two + rest, LANES), BF)]
    else:
        outs = [((end - begin, size_two, LANES), BF)] + [(one, F32) for one in sums]
    return pl.pallas_call(
        lambda *refs: after_kernel(scale, begin, reps if last else 0, *refs),
        grid_spec=pltpu.PrefetchScalarGridSpec(
            num_scalar_prefetch=1,
            grid=(end - begin,),
            in_specs=[
                whole(sorted_digits.shape),
                whole((total, width)),
                pl.BlockSpec((D1 * R, group), lambda k, o: (0, begin + k)),
                pl.BlockSpec((D3 * R, group), lambda k, o: (0, begin + k)),
                pl.BlockSpec((D1 * D2 * R, group), lambda k, o: (0, begin + k)),
                pl.BlockSpec((1, R, D2 * R), lambda k, o: (begin + k, 0, 0)),
            ]
            + extra_in,
            out_specs=[whole(shape) for shape, kind in outs],
            scratch_shapes=[
                pltpu.VMEM((total, width), F32),
                pltpu.VMEM((2, group, width), F32),
                pltpu.VMEM((width, group), F32),
                pltpu.VMEM((D1 * D2 * R, group), BF),
                pltpu.VMEM((D3 * R, group), BF),
                pltpu.VMEM((D1 * R, I1), F32),
                pltpu.VMEM((D3 * R, I3), F32),
            ],
        ),
        out_shape=[jax.ShapeDtypeStruct(*one) for one in outs],
        compiler_params=pltpu.CompilerParams(vmem_limit_bytes=48 << 20),
        name="after",
    )(order, sorted_digits, received, left, right, chained, core_two, *old)


CUT = 8
AXES = {"x": 4, "z_hi": 2, "core": 2, "y": 4, "z_lo": 8}


def groups_of(*names):
    places = np.arange(int(np.prod(list(AXES.values())))).reshape(tuple(AXES.values()))
    order = list(AXES)
    moved = [order.index(n) for n in names]
    kept = [i for i in range(len(order)) if i not in moved]
    return places.transpose(kept + moved).reshape(-1, int(np.prod([AXES[n] for n in names]))).tolist()


def swap(array, *names):
    return lax.all_to_all(
        array, ("rep", "tab"), 0, 0, axis_index_groups=groups_of(*names), tiled=True
    )


def add_up(array, *names):
    return jnp.sum(swap(array, *names).astype(F32), axis=0)


def shift(array, axis, by):
    size = 4
    step = 4 if axis == "rep" else 8
    number = size * step
    return lax.ppermute(array, axis, [(i, (i + by * step) % number) for i in range(number)])


def swap_core(array):
    return lax.ppermute(array, "rep", [(i, i ^ 1) for i in range(16)])


def gather_up(array, size, *names):
    return swap(jnp.broadcast_to(array[None], (size,) + array.shape), *names)


def on_device(
    bottom_out,
    pooled,
    top_grad,
    top_weight,
    core_first,
    core_mid,
    core_last,
    digit_first,
    digit_last,
    grouped,
):
    samples, width = bottom_out.shape
    reps = lax.axis_size("rep")
    batch_all = samples * reps * lax.axis_size("tab")
    scale = float(np.float32(1.0 / np.sqrt(batch_all)))
    grad_rows, grad_bottom, feat = dense(bottom_out, pooled, top_grad, top_weight)
    received = lax.all_to_all(grad_rows, "tab", split_axis=0, concat_axis=0, tiled=True)
    rep, tab = lax.axis_index("rep"), lax.axis_index("tab")
    where = jnp.stack([rep >> 2, rep & 1, tab >> 3, rep >> 1 & 1]).astype(jnp.int32)
    rows = top_weight.shape[0]
    padded = -(-rows // 2 // 64) * 64
    quarter = padded // 4
    keep, send = gram(where, feat, top_grad, scale, (4, padded, LANES))
    own, *others = join_core(keep, swap_core(send))
    order, own, others = lax.optimization_barrier((grouped[0, 0], own, others))
    sorted_digits, links = before(
        order, digit_first[0], digit_last[0], core_first[0], core_mid[0], core_last[0]
    )
    own, *others = join_x(where, own, *[shift(one, "rep", 1 + n) for n, one in enumerate(others)])
    partial = join_y(own, *[shift(one, "tab", 1 + n) for n, one in enumerate(others)])
    received = received.reshape(-1, width)
    links, partial = lax.optimization_barrier((links, partial))
    received, partial = lax.optimization_barrier((received, partial))

    def piece(begin, end, old):
        return after(begin, end, received, order, sorted_digits, links, core_mid[0], scale, reps, old)

    two, one, three = piece(0, CUT, ())
    summed = join_z(swap(partial, "z_hi", "z_lo"))
    one, summed = lax.optimization_barrier((one, summed))
    (parts,) = piece(CUT, I2, (one, three, two))
    mine = swap(summed, "x", "y").reshape(4, padded, LANES)
    parts, mine = lax.optimization_barrier((parts, mine))
    parts = add_up(parts.reshape(2, 8, -1, LANES), "core").astype(BF)
    parts = add_up(parts.reshape(4, 2, -1, LANES), "x")
    other_mine = swap_core(mine)
    parts, other_mine = lax.optimization_barrier((parts, other_mine))
    sent = jnp.where(where[3] == 0, parts[1], parts[0]).astype(BF)
    other = lax.ppermute(sent, "rep", [(i, i ^ 2) for i in range(16)])
    grad_top = assemble(where, (rows, top_grad.shape[1]), mine, other_mine)
    grad_one, grad_two, grad_three = last_sum(where, parts, other, reps)
    grad_one, grad_two, grad_three = grad_one[None], grad_two[None, None], grad_three[None]
    return (grad_one, grad_two, grad_three, grad_top, grad_bottom)


def solution(mesh):
    return jax.shard_map(
        on_device,
        mesh=mesh,
        in_specs=(
            P(("rep", "tab"), None),
            P(("rep", "tab"), None, None),
            P(("rep", "tab"), None),
            P(),
            P("tab", None, None),
            P("tab", None, None, None),
            P("tab", None, None),
            P("tab", "rep"),
            P("tab", "rep"),
            P("tab", "rep", None),
        ),
        out_specs=(
            P("tab", "rep", None),
            P("tab", "rep", None, None),
            P("tab", "rep", None),
            P(),
            P(("rep", "tab"), None),
        ),
        check_vma=False,
    )
```
